256 devices in a mesh: fine: 8 (over z_hi, core), coarse: 32 (over x, y, z_lo).
Axes of the slice: x: 4, y: 4, z: 8 (z_hi: 4, z_lo: 2; z = z_hi * 2 + z_lo), core: 2. Of those that a mesh axis runs over, the one named last changes fastest.
Arguments:
- query_rows: bfloat16 [32, 8, 128, 3072], P('coarse', 'fine'), may hold values from -5 to 5
- key_rows: bfloat16 [32, 8, 128, 3072], P('coarse', 'fine'), may hold values from -5 to 5
- value_rows: bfloat16 [32, 8, 128, 3072], P('coarse', 'fine'), may hold values from -5 to 5
- out_grad: bfloat16 [32, 8, 128, 3072], P('coarse', 'fine'), may hold values from -5 to 5
Outputs:
- attended: bfloat16 [32, 8, 128, 3072], P('coarse', 'fine')
- query_grad: bfloat16 [32, 8, 128, 3072], P('coarse', 'fine')
- key_grad: bfloat16 [32, 8, 128, 3072], P('coarse', 'fine')
- value_grad: bfloat16 [32, 8, 128, 3072], P('coarse', 'fine')
The draws below stay inside these ranges and needn't reach their ends.
All inputs are finite; a program needn't handle non-finite values.
Results may differ from the reference program's by a relative error of at most 0.0079.
Values may be sent and summed in bfloat16 or wider, within the bound.
No kernel may reach another device: no remote copies, remote signals or barrier semaphores. Data moves between devices by JAX's collectives and lax.ppermute only.
A program may use at most 128 MiB of HBM per device.

```python
import jax
import jax.numpy as jnp
from jax import lax

HEADS = 24
HEAD_DIM = 128
BLOCK = 256
LEVELS = 3
WIDTH = 3072
TOK_DEV = 128
OUTER_SEGS = 32
INNER_SEGS = 8
TOKENS = 32768


def draw_query_rows(key, part):
    key = jax.random.fold_in(key, 1)
    drawn = jnp.clip(jax.random.normal(key, (TOKENS, WIDTH)), -5.0, 5.0)
    return drawn.reshape(OUTER_SEGS, INNER_SEGS, TOK_DEV, WIDTH).astype(jnp.bfloat16)


def draw_key_rows(key, part):
    key = jax.random.fold_in(key, 2)
    drawn = jnp.clip(jax.random.normal(key, (TOKENS, WIDTH)), -5.0, 5.0)
    return drawn.reshape(OUTER_SEGS, INNER_SEGS, TOK_DEV, WIDTH).astype(jnp.bfloat16)


def shard_levels(key, dims, shards, smallest, top_value):
    gain, own = 1.0, jax.random.fold_in(key, 6)
    for axis_at, blocks in shards:
        steps = jnp.exp(jax.random.uniform(jax.random.fold_in(own, axis_at), (blocks,), jnp.float32, smallest / len(shards), top_value / len(shards)))
        gain = gain * jnp.repeat(steps, dims[axis_at] // blocks).reshape([-1 if axis == axis_at else 1 for axis in range(len(dims))])
    return gain


def bell_draw(rng, shape, deviation, limit, cuts=(), dtype=jnp.bfloat16):
    values = jax.random.normal(rng, shape, jnp.float32) * deviation
    if len(cuts) > 0:
        values = shard_levels(rng, shape, cuts, -0.22, 0.18) * values
    return jnp.clip(values, min=-limit, max=limit).astype(dtype)


def setup_inputs(seed: int = 0) -> dict:
    seeds = jax.random.split(jax.random.key(seed), 5)
    return {
        "query_rows": draw_query_rows(jax.random.fold_in(seeds[4], 71), 0),
        "key_rows": draw_key_rows(jax.random.fold_in(seeds[4], 71), 0),
        "value_rows": bell_draw(seeds[2], (OUTER_SEGS, INNER_SEGS, TOK_DEV, WIDTH), 1.0, 5.0, ((0, 32), (1, 8))),
        "out_grad": bell_draw(seeds[3], (OUTER_SEGS, INNER_SEGS, TOK_DEV, WIDTH), 1.0, 5.0, ((0, 32), (1, 8))),
    }


def coarse_rows(tok_rows, level_num):
    row_count, row_width = tok_rows.shape
    grouped = tok_rows.reshape(row_count // 2 ** level_num, 2 ** level_num, row_width)
    return (jnp.sum(grouped.astype(jnp.float32), axis=1) * (0.5 ** level_num)).astype(jnp.bfloat16)


def sibling_rows(coarse, level_num):
    half_rows = BLOCK // 2
    row_width = coarse.shape[-1]
    flipped = coarse.reshape(-1, 2, half_rows, row_width)[:, ::-1]
    return jnp.repeat(flipped.reshape(-1, half_rows, row_width), 2 ** (level_num - 1), axis=0)


def return_rows(grad_terms, level_num):
    half_rows = grad_terms.shape[1]
    row_width = grad_terms.shape[2]
    summed = jnp.sum(grad_terms.reshape(-1, 2 ** (level_num - 1), half_rows, row_width), axis=1)
    owned = summed.reshape(-1, 2, half_rows, row_width)[:, ::-1].reshape(-1, row_width)
    return jnp.repeat(owned, 2 ** level_num, axis=0) * (0.5 ** level_num)


def attend_block(block_items):
    query_block, key_set, value_set, grad_block = block_items
    highest = lax.Precision.HIGHEST
    score_scale = HEAD_DIM ** -0.5
    query_heads = query_block.reshape(-1, HEADS, HEAD_DIM).astype(jnp.float32)
    key_heads = key_set.reshape(-1, HEADS, HEAD_DIM).astype(jnp.float32)
    value_heads = value_set.reshape(-1, HEADS, HEAD_DIM).astype(jnp.float32)
    grad_heads = grad_block.reshape(-1, HEADS, HEAD_DIM).astype(jnp.float32)
    scores = jnp.einsum("qhd,khd->hqk", query_heads, key_heads, precision=highest) * score_scale
    row_max = jnp.max(scores, axis=-1, keepdims=True)
    exp_scores = jnp.exp(scores - row_max)
    weights = exp_scores / jnp.sum(exp_scores, axis=-1, keepdims=True)
    weights_low = lax.optimization_barrier(weights.astype(jnp.bfloat16)).astype(jnp.float32)
    attended = jnp.einsum("hqk,khd->qhd", weights_low, value_heads, precision=highest)
    prob_grad = jnp.einsum("qhd,khd->hqk", grad_heads, value_heads, precision=highest)
    row_inner = jnp.sum(weights * prob_grad, axis=-1, keepdims=True)
    score_grad = lax.optimization_barrier((weights * (prob_grad - row_inner)).astype(jnp.bfloat16)).astype(jnp.float32)
    query_grad = jnp.einsum("hqk,khd->qhd", score_grad, key_heads, precision=highest) * score_scale
    key_terms = jnp.einsum("hqk,qhd->khd", score_grad, query_heads, precision=highest) * score_scale
    value_terms = jnp.einsum("hqk,qhd->khd", weights_low, grad_heads, precision=highest)
    row_count = query_block.shape[0]
    row_width = query_block.shape[1]
    return (attended.reshape(row_count, row_width).astype(jnp.bfloat16),
            query_grad.reshape(row_count, row_width).astype(jnp.bfloat16),
            key_terms.reshape(-1, row_width),
            value_terms.reshape(-1, row_width))


def reference(query_rows, key_rows, value_rows, out_grad):
    full_shape = query_rows.shape
    row_width = full_shape[-1]
    queries = query_rows.reshape(-1, row_width)
    keys_flat = key_rows.reshape(-1, row_width)
    values_flat = value_rows.reshape(-1, row_width)
    grads_flat = out_grad.reshape(-1, row_width)
    blocks = queries.shape[0] // BLOCK
    key_parts = [keys_flat.reshape(blocks, BLOCK, row_width)]
    value_parts = [values_flat.reshape(blocks, BLOCK, row_width)]
    for level_num in range(1, LEVELS + 1):
        key_parts.append(sibling_rows(coarse_rows(keys_flat, level_num), level_num))
        value_parts.append(sibling_rows(coarse_rows(values_flat, level_num), level_num))
    key_set = jnp.concatenate(key_parts, axis=1)
    value_set = jnp.concatenate(value_parts, axis=1)
    attended, query_grad, key_terms, value_terms = lax.map(
        attend_block,
        (queries.reshape(blocks, BLOCK, row_width), key_set, value_set, grads_flat.reshape(blocks, BLOCK, row_width)))
    key_total = key_terms[:, :BLOCK].reshape(-1, row_width)
    value_total = value_terms[:, :BLOCK].reshape(-1, row_width)
    half_rows = BLOCK // 2
    for level_num in range(1, LEVELS + 1):
        low_edge = BLOCK + (level_num - 1) * half_rows
        key_total = key_total + return_rows(key_terms[:, low_edge:low_edge + half_rows], level_num)
        value_total = value_total + return_rows(value_terms[:, low_edge:low_edge + half_rows], level_num)
    return (attended.reshape(full_shape), query_grad.reshape(full_shape),
            key_total.astype(jnp.bfloat16).reshape(full_shape),
            value_total.astype(jnp.bfloat16).reshape(full_shape))
```

```python
import functools
import math

import jax
import jax.numpy as jnp
from jax import lax
from jax.experimental import pallas as pl
from jax.experimental.pallas import tpu as pltpu
from jax.sharding import PartitionSpec as P

HEADS = 24
HEAD_DIM = 128
ROWS = 128
BLOCK = 256
CORE_HEADS = HEADS // 2
HALF = CORE_HEADS * HEAD_DIM
SCALE = HEAD_DIM**-0.5
EXP2_SCALE = SCALE * math.log2(math.e)
CHUNKS = (3, 3, 3, 3)
VMEM_LIMIT = 40 * 2**20
BF16 = jnp.bfloat16
F32 = jnp.float32


def params(steps=1):
    return pltpu.CompilerParams(
        dimension_semantics=("arbitrary",) * steps, vmem_limit_bytes=VMEM_LIMIT
    )


def averager(rows, group):
    row = lax.broadcasted_iota(jnp.int32, (rows, rows * group), 0)
    col = lax.broadcasted_iota(jnp.int32, (rows, rows * group), 1)
    return jnp.where(col // group == row, 1.0 / group, 0.0).astype(BF16)


def spreader(rows, group):
    row = lax.broadcasted_iota(jnp.int32, (rows * group, rows), 0)
    col = lax.broadcasted_iota(jnp.int32, (rows * group, rows), 1)
    return jnp.where(row // group == col, 1.0 / group, 0.0).astype(BF16)


def dot(a, b, dims=((1,), (0,))):
    return lax.dot_general(a, b, (dims, ((), ())), preferred_element_type=F32)


def extract_kernel(core, a_ref, b_ref, out_ref):
    out_ref[0] = a_ref[...]
    out_ref[1] = b_ref[...]


def extract_other(core, a, b):
    half = pl.BlockSpec((ROWS, HALF), lambda i, c: (0, 1 - c[0]))
    return pl.pallas_call(
        extract_kernel,
        grid_spec=pltpu.PrefetchScalarGridSpec(
            num_scalar_prefetch=1,
            grid=(1,),
            in_specs=[half, half],
            out_specs=pl.BlockSpec((2, ROWS, HALF), lambda i, c: (0, 0, 0)),
        ),
        out_shape=jax.ShapeDtypeStruct((2, ROWS, HALF), BF16),
        compiler_params=params(),
        name="extract_other",
    )(core, a, b)


def pack_first_kernel(core, k_ref, v_ref, kv_ref, *outs):
    weights = jnp.concatenate(
        [averager(BLOCK >> level, 1 << level) for level in (1, 2, 3)], axis=0
    )
    for part, own in enumerate((k_ref, v_ref)):
        rows = jnp.concatenate([own[...], kv_ref[part]], axis=0)
        lane = 0
        for number in range(len(CHUNKS)):
            width = CHUNKS[number] * HEAD_DIM
            coarse = dot(weights, rows[:, lane : lane + width]).astype(BF16)
            outs[2 * number][part] = coarse[:128]
            outs[2 * number + 1][part] = coarse[128:]
            lane += width


def pack_first(core, keys, values, kv_recv):
    half = pl.BlockSpec((ROWS, HALF), lambda i, c: (0, c[0]))
    whole = pl.BlockSpec((2, ROWS, HALF), lambda i, c: (0, 0, 0))
    out_specs, out_shape = [], []
    for heads in CHUNKS:
        for count in (128, 96):
            shape = (2, count, heads * HEAD_DIM)
            out_specs.append(pl.BlockSpec(shape, lambda i, c: (0, 0, 0)))
            out_shape.append(jax.ShapeDtypeStruct(shape, BF16))
    return pl.pallas_call(
        pack_first_kernel,
        grid_spec=pltpu.PrefetchScalarGridSpec(
            num_scalar_prefetch=1, grid=(1,), in_specs=[half, half, whole], out_specs=out_specs
        ),
        out_shape=out_shape,
        compiler_params=params(),
        name="pack_first",
    )(core, keys, values, kv_recv)


def whole_call(kernel, name, out_shape, *args):
    return pl.pallas_call(
        kernel,
        in_specs=[pl.BlockSpec(memory_space=pltpu.VMEM)] * len(args),
        out_specs=pl.BlockSpec(memory_space=pltpu.VMEM),
        out_shape=out_shape,
        compiler_params=pltpu.CompilerParams(vmem_limit_bytes=VMEM_LIMIT),
        name=name,
    )(*args)


def pack_second_kernel(own_ref, first_ref, out_ref):
    pairs = averager(64, 2)
    for part in range(2):
        out_ref[part, :64] = own_ref[part, :64]
        out_ref[part, 64:] = dot(pairs, first_ref[part]).astype(BF16)


def pack_third_kernel(own_ref, first_ref, second_ref, out_ref):
    fours = averager(32, 4)
    pairs = averager(64, 2)
    for part in range(2):
        out_ref[part, :32] = own_ref[part, 64:]
        out_ref[part, 32:64] = dot(fours, first_ref[part]).astype(BF16)
        out_ref[part, 64:] = dot(pairs, second_ref[part]).astype(BF16)


def attend_kernel(
    core, q_own, g_own, k_own, v_own, qg_recv, kv_recv, first, second, third, *refs
):
    own_out, peer_out, exact_out, first_out, second_out, third_out = refs[-6:]
    queries = jnp.concatenate([q_own[...], qg_recv[0]], axis=0)
    grads = jnp.concatenate([g_own[...], qg_recv[1]], axis=0)
    keys = jnp.concatenate([k_own[...], kv_recv[0], first[0], second[0], third[0]], axis=0)
    values = jnp.concatenate([v_own[...], kv_recv[1], first[1], second[1], third[1]], axis=0)
    scores = dot(keys, queries, ((1,), (1,)))
    row_max = jnp.max(scores, axis=0, keepdims=True)
    exp_scores = jnp.exp2((scores - row_max) * EXP2_SCALE)
    weights = exp_scores * (1.0 / jnp.sum(exp_scores, axis=0, keepdims=True))
    weights_low = weights.astype(BF16)
    prob_grad = dot(values, grads, ((1,), (1,)))
    row_inner = jnp.sum(weights * prob_grad, axis=0, keepdims=True)
    score_grad = (weights * (prob_grad - row_inner)).astype(BF16)
    attended = dot(values.T, weights_low).T
    query_grad = dot(keys.T, score_grad).T * SCALE
    for part, result in enumerate((attended, query_grad)):
        result = result.astype(BF16)
        own_out[part] = result[:ROWS]
        peer_out[part] = result[ROWS:]
    key_terms = dot(score_grad, queries) * SCALE
    value_terms = dot(weights_low, grads)
    for part, terms in enumerate((key_terms, value_terms)):
        exact_out[part] = terms[:256]
        first_out[part] = terms[256:384]
        second_out[part] = terms[384:512]
        third_out[part] = terms[512:].astype(BF16)


def attend(core, start, heads, q, g, k, v, qg_recv, kv_recv, first, second, third, chain):
    own = pl.BlockSpec((ROWS, HEAD_DIM), lambda h, c: (0, c[0] * CORE_HEADS + start + h))
    recv = pl.BlockSpec((2, ROWS, HEAD_DIM), lambda h, c: (0, 0, start + h))
    local = pl.BlockSpec((2, ROWS, HEAD_DIM), lambda h, c: (0, 0, h))
    local_exact = pl.BlockSpec((2, BLOCK, HEAD_DIM), lambda h, c: (0, 0, h))
    anywhere = pl.BlockSpec(memory_space=pl.ANY)
    width = heads * HEAD_DIM
    ops = 6 * 2 * 256 * 640 * 128 * heads
    chain = list(chain) if chain is not None else []
    return pl.pallas_call(
        attend_kernel,
        grid_spec=pltpu.PrefetchScalarGridSpec(
            num_scalar_prefetch=1,
            grid=(heads,),
            in_specs=[own] * 4 + [recv] * 2 + [local] * 3 + [anywhere] * len(chain),
            out_specs=[recv, recv, local_exact, local, local, local],
        ),
        out_shape=[
            jax.ShapeDtypeStruct((2, ROWS, HALF), BF16),
            jax.ShapeDtypeStruct((2, ROWS, HALF), BF16),
            jax.ShapeDtypeStruct((2, BLOCK, width), F32),
            jax.ShapeDtypeStruct((2, ROWS, width), F32),
            jax.ShapeDtypeStruct((2, ROWS, width), F32),
            jax.ShapeDtypeStruct((2, ROWS, width), BF16),
        ],
        input_output_aliases={10: 0, 11: 1} if chain else {},
        compiler_params=params(),
        cost_estimate=pl.CostEstimate(
            flops=2 * ops, bytes_accessed=20 * 128 * 2 * width, transcendentals=256 * 640 * heads
        ),
        name="attend",
    )(core, q, g, k, v, qg_recv, kv_recv, first, second, third, *chain)


def back_second_kernel(second_ref, third_ref, out_ref):
    pairs = spreader(64, 2)
    for part in range(2):
        out_ref[part] = (second_ref[part] + dot(pairs, third_ref[part, 64:])).astype(BF16)


def back_first_kernel(first_ref, second_ref, third_ref, out_ref):
    pairs = spreader(64, 2)
    fours = spreader(32, 4)
    for part in range(2):
        out_ref[part] = (
            first_ref[part]
            + dot(pairs, second_ref[part, 64:])
            + dot(fours, third_ref[part, 32:64])
        ).astype(BF16)


def finish_kernel(exact_ref, first_ref, second_ref, third_ref, *refs):
    own_out, peer_out = refs[-2:]
    for part in range(2):
        total = (
            exact_ref[part]
            + dot(spreader(128, 2), first_ref[part])
            + dot(spreader(64, 4), second_ref[part, :64])
            + dot(spreader(32, 8), third_ref[part, :32])
        ).astype(BF16)
        own_out[part] = total[:ROWS]
        peer_out[part] = total[ROWS:]


def finish(start, heads, exact, first, second, third, chain):
    local = pl.BlockSpec((2, ROWS, HEAD_DIM), lambda h: (0, 0, h))
    local_exact = pl.BlockSpec((2, BLOCK, HEAD_DIM), lambda h: (0, 0, h))
    placed = pl.BlockSpec((2, ROWS, HEAD_DIM), lambda h: (0, 0, start + h))
    anywhere = pl.BlockSpec(memory_space=pl.ANY)
    chain = list(chain) if chain is not None else []
    return pl.pallas_call(
        finish_kernel,
        grid=(heads,),
        in_specs=[local_exact, local, local, local] + [anywhere] * len(chain),
        out_specs=[placed, placed],
        out_shape=[jax.ShapeDtypeStruct((2, ROWS, HALF), BF16)] * 2,
        input_output_aliases={4: 0, 5: 1} if chain else {},
        compiler_params=params(),
        name="finish",
    )(exact, first, second, third, *chain)


def assemble_kernel(core, own_ref, recv_ref, a_ref, b_ref):
    mine = pl.program_id(0) == core[0]

    @pl.when(mine)
    def _():
        a_ref[...] = own_ref[0]
        b_ref[...] = own_ref[1]

    @pl.when(jnp.logical_not(mine))
    def _():
        a_ref[...] = recv_ref[0]
        b_ref[...] = recv_ref[1]


def assemble(core, own, recv):
    whole = pl.BlockSpec((2, ROWS, HALF), lambda j, c: (0, 0, 0))
    half = pl.BlockSpec((ROWS, HALF), lambda j, c: (0, j))
    return pl.pallas_call(
        assemble_kernel,
        grid_spec=pltpu.PrefetchScalarGridSpec(
            num_scalar_prefetch=1, grid=(2,), in_specs=[whole, whole], out_specs=[half, half]
        ),
        out_shape=[jax.ShapeDtypeStruct((ROWS, 2 * HALF), BF16)] * 2,
        compiler_params=params(),
        name="assemble",
    )(core, own, recv)


def swap_core(block):
    return lax.ppermute(block, "fine", [(i, i ^ 1) for i in range(lax.axis_size("fine"))])


def swap_fine(block, mask):
    return lax.ppermute(block, "fine", [(i, i ^ mask) for i in range(lax.axis_size("fine"))])


def swap_next(block, odd):
    fine, coarse = lax.axis_size("fine"), lax.axis_size("coarse")
    route = []
    for f in range(fine):
        for c in range(coarse):
            z = (f // 2) * 2 + c % 2
            if odd:
                there = (z + 1 if z % 2 else z - 1) % fine
            else:
                there = z ^ 1
            route.append((f * coarse + c, (there // 2 * 2 + f % 2) * coarse + c - c % 2 + there % 2))
    return lax.ppermute(block, ("fine", "coarse"), route)


def body(query_rows, key_rows, value_rows, out_grad):
    full_shape = query_rows.shape
    queries, keys, values, grads = (
        block.reshape(ROWS, 2 * HALF) for block in (query_rows, key_rows, value_rows, out_grad)
    )
    core = (lax.axis_index("fine") % 2).astype(jnp.int32).reshape(1)
    kv_recv = swap_core(extract_other(core, keys, values))
    qg_recv = swap_core(extract_other(core, queries, grads))
    packed = pack_first(core, keys, values, kv_recv)
    count = len(CHUNKS)
    starts = [sum(CHUNKS[:n]) for n in range(count)]
    first, second, third = [None] * count, [None] * count, [None] * count
    results = [None] * count
    third_back, second_back, first_back = [None] * count, [None] * count, [None] * count
    own_packed = [packed[2 * n + 1] for n in range(count)]
    a_chain, b_chain = None, None

    def shape_of(n, rows=ROWS):
        return jax.ShapeDtypeStruct((2, rows, CHUNKS[n] * HEAD_DIM), BF16)

    for n in range(count):
        first[n] = swap_fine(packed[2 * n], 2)
    for n in range(count):
        send = whole_call(pack_second_kernel, "pack_second", shape_of(n), own_packed[n], first[n])
        second[n] = swap_fine(send, 6)
    for n in range(count):
        send = whole_call(
            pack_third_kernel, "pack_third", shape_of(n), own_packed[n], first[n], second[n]
        )
        third[n] = swap_next(send, n % 2)
    for n in range(count):
        results[n] = attend(
            core, starts[n], CHUNKS[n], queries, grads, keys, values, qg_recv, kv_recv,
            first[n], second[n], third[n], a_chain,
        )
        a_chain = results[n][:2]
        third_back[n] = swap_next(results[n][5], n % 2)
    a_recv = swap_core(a_chain[1])
    for n in range(count):
        send = whole_call(back_second_kernel, "back_second", shape_of(n), results[n][4], third_back[n])
        second_back[n] = swap_fine(send, 6)
    attended, query_grad = assemble(core, a_chain[0], a_recv)
    for n in range(count):
        send = whole_call(
            back_first_kernel, "back_first", shape_of(n), results[n][3], second_back[n], third_back[n]
        )
        first_back[n] = swap_fine(send, 2)
    for n in range(count):
        b_chain = finish(
            starts[n], CHUNKS[n], results[n][2], first_back[n], second_back[n], third_back[n], b_chain
        )
    b_recv = swap_core(b_chain[1])
    key_grad, value_grad = assemble(core, b_chain[0], b_recv)
    return tuple(
        block.reshape(full_shape) for block in (attended, query_grad, key_grad, value_grad)
    )


def solution(mesh):
    placed = P("coarse", "fine", None, None)
    return jax.shard_map(
        body, mesh=mesh, in_specs=(placed,) * 4, out_specs=(placed,) * 4, check_vma=False
    )
```

```python
import functools
import math

import jax
import jax.numpy as jnp
from jax import lax
from jax.experimental import pallas as pl
from jax.experimental.pallas import tpu as pltpu
from jax.sharding import PartitionSpec as P

HEADS = 24
HEAD_DIM = 128
ROWS = 128
BLOCK = 256
CORE_HEADS = HEADS // 2
HALF = CORE_HEADS * HEAD_DIM
SCALE = HEAD_DIM**-0.5
EXP2_SCALE = SCALE * math.log2(math.e)
COST = pl.CostEstimate(flops=1, bytes_accessed=1, transcendentals=0)
CHUNKS = (3, 3, 3, 3)
PARITY = (0, 1, 0, 1)
ORDER = (
    "K0", "A0", "Q0", "A1", "B0", "A2", "B1", "D0", "A3", "B2",
    "D1", "E0", "B3", "D2", "E1", "F0", "D3", "E2", "F1", "G0",
    "E3", "S0", "F2", "G1", "F3", "H0", "G2", "H1", "G3", "H2",
    "T0", "H3",
)
VMEM_LIMIT = 40 * 2**20
BF16 = jnp.bfloat16
F32 = jnp.float32
ANYWHERE = pl.BlockSpec(memory_space=pl.ANY)


def params(steps=1):
    return pltpu.CompilerParams(
        dimension_semantics=("arbitrary",) * steps, vmem_limit_bytes=VMEM_LIMIT
    )


def averager(rows, group):
    row = lax.broadcasted_iota(jnp.int32, (rows, rows * group), 0)
    col = lax.broadcasted_iota(jnp.int32, (rows, rows * group), 1)
    return jnp.where(col // group == row, 1.0 / group, 0.0).astype(BF16)


def spreader(rows, group):
    row = lax.broadcasted_iota(jnp.int32, (rows * group, rows), 0)
    col = lax.broadcasted_iota(jnp.int32, (rows * group, rows), 1)
    return jnp.where(row // group == col, 1.0 / group, 0.0).astype(BF16)


def dot(a, b, dims=((1,), (0,))):
    return lax.dot_general(a, b, (dims, ((), ())), preferred_element_type=F32)


def extract_kernel(core, a_ref, b_ref, *refs):
    out_ref = refs[-1]
    out_ref[0] = a_ref[...]
    out_ref[1] = b_ref[...]


def extract_other(core, a, b, after, limit):
    half = pl.BlockSpec((ROWS, HALF), lambda i, c: (0, 1 - c[0]))
    return pl.pallas_call(
        extract_kernel,
        grid_spec=pltpu.PrefetchScalarGridSpec(
            num_scalar_prefetch=1,
            grid=(1,),
            in_specs=[half, half] + [ANYWHERE] * len(after),
            out_specs=pl.BlockSpec((2, ROWS, HALF), lambda i, c: (0, 0, 0)),
        ),
        out_shape=jax.ShapeDtypeStruct((2, ROWS, HALF), BF16),
        cost_estimate=COST,
        compiler_params=pltpu.CompilerParams(vmem_limit_bytes=limit),
        name="extract_other",
    )(core, a, b, *after)


def pack_first_kernel(core, k_ref, v_ref, kv_ref, *refs):
    first_out, own_out = refs[-2:]
    weights = jnp.concatenate(
        [averager(BLOCK >> level, 1 << level) for level in (1, 2, 3)], axis=0
    )
    for part, own in enumerate((k_ref, v_ref)):
        rows = jnp.concatenate([own[...], kv_ref[part]], axis=0)
        coarse = dot(weights, rows).astype(BF16)
        first_out[part] = coarse[:128]
        own_out[part] = coarse[128:]


def pack_first(core, start, heads, keys, values, kv_recv, after):
    own = pl.BlockSpec((ROWS, HEAD_DIM), lambda h, c: (0, c[0] * CORE_HEADS + start + h))
    recv = pl.BlockSpec((2, ROWS, HEAD_DIM), lambda h, c: (0, 0, start + h))
    return pl.pallas_call(
        pack_first_kernel,
        grid_spec=pltpu.PrefetchScalarGridSpec(
            num_scalar_prefetch=1,
            grid=(heads,),
            in_specs=[own, own, recv] + [ANYWHERE] * len(after),
            out_specs=[
                pl.BlockSpec((2, count, HEAD_DIM), lambda h, c: (0, 0, h)) for count in (128, 96)
            ],
        ),
        out_shape=[
            jax.ShapeDtypeStruct((2, count, heads * HEAD_DIM), BF16) for count in (128, 96)
        ],
        cost_estimate=COST,
        compiler_params=params(),
        name="pack_first",
    )(core, keys, values, kv_recv, *after)


def whole_call(kernel, name, out_shape, after, *args):
    return pl.pallas_call(
        kernel,
        in_specs=[pl.BlockSpec(memory_space=pltpu.VMEM)] * len(args) + [ANYWHERE] * len(after),
        out_specs=pl.BlockSpec(memory_space=pltpu.VMEM),
        out_shape=out_shape,
        cost_estimate=COST,
        compiler_params=pltpu.CompilerParams(vmem_limit_bytes=VMEM_LIMIT),
        name=name,
    )(*args, *after)


def pack_second_kernel(own_ref, first_ref, *refs):
    out_ref = refs[-1]
    pairs = averager(64, 2)
    for part in range(2):
        out_ref[part, :64] = own_ref[part, :64]
        out_ref[part, 64:] = dot(pairs, first_ref[part]).astype(BF16)


def pack_third_kernel(own_ref, first_ref, second_ref, *refs):
    out_ref = refs[-1]
    fours = averager(32, 4)
    pairs = averager(64, 2)
    for part in range(2):
        out_ref[part, :32] = own_ref[part, 64:]
        out_ref[part, 32:64] = dot(fours, first_ref[part]).astype(BF16)
        out_ref[part, 64:] = dot(pairs, second_ref[part]).astype(BF16)


def attend_kernel(
    core, q_own, g_own, k_own, v_own, qg_recv, kv_recv, first, second, third, *refs
):
    own_out, peer_out, exact_out, first_out, second_out, third_out = refs[-6:]
    queries = jnp.concatenate([q_own[...], qg_recv[0]], axis=0)
    grads = jnp.concatenate([g_own[...], qg_recv[1]], axis=0)
    keys = jnp.concatenate([k_own[...], kv_recv[0], first[0], second[0], third[0]], axis=0)
    values = jnp.concatenate([v_own[...], kv_recv[1], first[1], second[1], third[1]], axis=0)
    scores = dot(keys, queries, ((1,), (1,)))
    row_max = jnp.max(scores, axis=0, keepdims=True)
    exp_scores = jnp.exp2((scores - row_max) * EXP2_SCALE)
    weights = exp_scores * (1.0 / jnp.sum(exp_scores, axis=0, keepdims=True))
    weights_low = weights.astype(BF16)
    prob_grad = dot(values, grads, ((1,), (1,)))
    row_inner = jnp.sum(weights * prob_grad, axis=0, keepdims=True)
    score_grad = (weights * (prob_grad - row_inner)).astype(BF16)
    attended = dot(values.T, weights_low).T
    query_grad = dot(keys.T, score_grad).T * SCALE
    for part, result in enumerate((attended, query_grad)):
        result = result.astype(BF16)
        own_out[part] = result[:ROWS]
        peer_out[part] = result[ROWS:]
    key_terms = dot(score_grad, queries) * SCALE
    value_terms = dot(weights_low, grads)
    for part, terms in enumerate((key_terms, value_terms)):
        exact_out[part] = terms[:256]
        first_out[part] = terms[256:384]
        second_out[part] = terms[384:512]
        third_out[part] = terms[512:].astype(BF16)


def attend(core, start, heads, q, g, k, v, qg_recv, kv_recv, first, second, third, chain, after):
    own = pl.BlockSpec((ROWS, HEAD_DIM), lambda h, c: (0, c[0] * CORE_HEADS + start + h))
    recv = pl.BlockSpec((2, ROWS, HEAD_DIM), lambda h, c: (0, 0, start + h))
    local = pl.BlockSpec((2, ROWS, HEAD_DIM), lambda h, c: (0, 0, h))
    local_exact = pl.BlockSpec((2, BLOCK, HEAD_DIM), lambda h, c: (0, 0, h))
    width = heads * HEAD_DIM
    ops = 6 * 2 * 256 * 640 * 128 * heads
    chain = list(chain) if chain is not None else []
    return pl.pallas_call(
        attend_kernel,
        grid_spec=pltpu.PrefetchScalarGridSpec(
            num_scalar_prefetch=1,
            grid=(heads,),
            in_specs=[own] * 4 + [recv] * 2 + [local] * 3 + [ANYWHERE] * (len(chain) + len(after)),
            out_specs=[recv, recv, local_exact, local, local, local],
        ),
        out_shape=[
            jax.ShapeDtypeStruct((2, ROWS, HALF), BF16),
            jax.ShapeDtypeStruct((2, ROWS, HALF), BF16),
            jax.ShapeDtypeStruct((2, BLOCK, width), F32),
            jax.ShapeDtypeStruct((2, ROWS, width), F32),
            jax.ShapeDtypeStruct((2, ROWS, width), F32),
            jax.ShapeDtypeStruct((2, ROWS, width), BF16),
        ],
        input_output_aliases={10: 0, 11: 1} if chain else {},
        cost_estimate=COST,
        compiler_params=params(),
        name="attend",
    )(core, q, g, k, v, qg_recv, kv_recv, first, second, third, *chain, *after)


def back_second_kernel(second_ref, third_ref, *refs):
    out_ref = refs[-1]
    pairs = spreader(64, 2)
    for part in range(2):
        out_ref[part] = (second_ref[part] + dot(pairs, third_ref[part, 64:])).astype(BF16)


def back_first_kernel(first_ref, second_ref, third_ref, *refs):
    out_ref = refs[-1]
    pairs = spreader(64, 2)
    fours = spreader(32, 4)
    for part in range(2):
        out_ref[part] = (
            first_ref[part]
            + dot(pairs, second_ref[part, 64:])
            + dot(fours, third_ref[part, 32:64])
        ).astype(BF16)


def finish_kernel(exact_ref, first_ref, second_ref, third_ref, *refs):
    own_out, peer_out, token = refs[-3:]
    token[...] = jnp.zeros_like(token)
    for part in range(2):
        total = (
            exact_ref[part]
            + dot(spreader(128, 2), first_ref[part])
            + dot(spreader(64, 4), second_ref[part, :64])
            + dot(spreader(32, 8), third_ref[part, :32])
        ).astype(BF16)
        own_out[part] = total[:ROWS]
        peer_out[part] = total[ROWS:]


def finish(start, heads, exact, first, second, third, chain, after):
    local = pl.BlockSpec((2, ROWS, HEAD_DIM), lambda h: (0, 0, h))
    local_exact = pl.BlockSpec((2, BLOCK, HEAD_DIM), lambda h: (0, 0, h))
    placed = pl.BlockSpec((2, ROWS, HEAD_DIM), lambda h: (0, 0, start + h))
    chain = list(chain) if chain is not None else []
    return pl.pallas_call(
        finish_kernel,
        grid=(heads,),
        in_specs=[local_exact, local, local, local] + [ANYWHERE] * (len(chain) + len(after)),
        out_specs=[placed, placed, pl.BlockSpec((8, 128), lambda h: (0, 0))],
        out_shape=[jax.ShapeDtypeStruct((2, ROWS, HALF), BF16)] * 2
        + [jax.ShapeDtypeStruct((8, 128), F32)],
        input_output_aliases={4: 0, 5: 1} if chain else {},
        cost_estimate=COST,
        compiler_params=params(),
        name="finish",
    )(exact, first, second, third, *chain, *after)


def assemble_kernel(core, own_ref, recv_ref, *refs):
    a_ref, b_ref = refs[-2:]
    mine = pl.program_id(0) == core[0]

    @pl.when(mine)
    def _():
        a_ref[...] = own_ref[0]
        b_ref[...] = own_ref[1]

    @pl.when(jnp.logical_not(mine))
    def _():
        a_ref[...] = recv_ref[0]
        b_ref[...] = recv_ref[1]


def assemble(core, own, recv, after):
    whole = pl.BlockSpec((2, ROWS, HALF), lambda j, c: (0, 0, 0))
    half = pl.BlockSpec((ROWS, HALF), lambda j, c: (0, j))
    return pl.pallas_call(
        assemble_kernel,
        grid_spec=pltpu.PrefetchScalarGridSpec(
            num_scalar_prefetch=1, grid=(2,), in_specs=[whole, whole] + [ANYWHERE] * len(after), out_specs=[half, half]
        ),
        out_shape=[jax.ShapeDtypeStruct((ROWS, 2 * HALF), BF16)] * 2,
        cost_estimate=COST,
        compiler_params=params(),
        name="assemble",
    )(core, own, recv, *after)


def swap_core(block):
    return lax.ppermute(block, "fine", [(i, i ^ 1) for i in range(lax.axis_size("fine"))])


def swap_fine(block, mask):
    return lax.ppermute(block, "fine", [(i, i ^ mask) for i in range(lax.axis_size("fine"))])


def swap_next(block, odd):
    fine, coarse = lax.axis_size("fine"), lax.axis_size("coarse")
    route = []
    for f in range(fine):
        for c in range(coarse):
            z = (f // 2) * 2 + c % 2
            if odd:
                there = (z + 1 if z % 2 else z - 1) % fine
            else:
                there = z ^ 1
            route.append((f * coarse + c, (there // 2 * 2 + f % 2) * coarse + c - c % 2 + there % 2))
    return lax.ppermute(block, ("fine", "coarse"), route)


def body(query_rows, key_rows, value_rows, out_grad):
    full_shape = query_rows.shape
    queries, keys, values, grads = (
        block.reshape(ROWS, 2 * HALF) for block in (query_rows, key_rows, value_rows, out_grad)
    )
    core = (lax.axis_index("fine") % 2).astype(jnp.int32).reshape(1)
    count = len(CHUNKS)
    starts = [sum(CHUNKS[:n]) for n in range(count)]
    own_packed, first, second, third = ([None] * count for _ in range(4))
    results, third_back, second_back, first_back = ([None] * count for _ in range(4))
    a_chain, b_chain, a_recv, after = None, None, None, []

    def shape_of(n):
        return jax.ShapeDtypeStruct((2, ROWS, CHUNKS[n] * HEAD_DIM), BF16)

    for step in ORDER:
        kind, n = step[0], int(step[1:])
        if kind == "K":
            send = extract_other(core, keys, values, after, VMEM_LIMIT)
            kv_recv = swap_core(send)
        elif kind == "Q":
            send = extract_other(core, queries, grads, after, VMEM_LIMIT)
            qg_recv = swap_core(send)
        elif kind == "A":
            send, own_packed[n] = pack_first(core, starts[n], CHUNKS[n], keys, values, kv_recv, after)
            first[n] = swap_fine(send, 2)
        elif kind == "B":
            send = whole_call(
                pack_second_kernel, "pack_second", shape_of(n), after, own_packed[n], first[n]
            )
            second[n] = swap_fine(send, 6)
        elif kind == "D":
            send = whole_call(
                pack_third_kernel, "pack_third", shape_of(n), after, own_packed[n], first[n], second[n]
            )
            third[n] = swap_next(send, PARITY[n])
        elif kind == "E":
            results[n] = attend(
                core, starts[n], CHUNKS[n], queries, grads, keys, values, qg_recv, kv_recv,
                first[n], second[n], third[n], a_chain, after,
            )
            a_chain = results[n][:2]
            send = results[n][5]
            third_back[n] = swap_next(send, PARITY[n])
        elif kind == "F":
            send = whole_call(
                back_second_kernel, "back_second", shape_of(n), after, results[n][4], third_back[n]
            )
            second_back[n] = swap_fine(send, 6)
        elif kind == "G":
            send = whole_call(
                back_first_kernel, "back_first", shape_of(n), after,
                results[n][3], second_back[n], third_back[n],
            )
            first_back[n] = swap_fine(send, 2)
        elif kind == "H":
            *b_chain, send = finish(
                starts[n], CHUNKS[n], results[n][2], first_back[n], second_back[n], third_back[n],
                b_chain, after,
            )
        elif kind == "S":
            a_recv = swap_core(a_chain[1])
            continue
        elif kind == "R":
            after = after + [qg_recv]
            continue
        elif kind == "T":
            attended, query_grad = assemble(core, a_chain[0], a_recv, after)
            send = attended
        after = [send]
    b_recv = swap_core(b_chain[1])
    key_grad, value_grad = assemble(core, b_chain[0], b_recv, after)
    return tuple(
        block.reshape(full_shape) for block in (attended, query_grad, key_grad, value_grad)
    )


def solution(mesh):
    placed = P("coarse", "fine", None, None)
    return jax.shard_map(
        body, mesh=mesh, in_specs=(placed,) * 4, out_specs=(placed,) * 4, check_vma=False
    )
```

```python
import functools
import math

import jax
import jax.numpy as jnp
from jax import lax
from jax.experimental import pallas as pl
from jax.experimental.pallas import tpu as pltpu
from jax.sharding import PartitionSpec as P

HEADS = 24
HEAD_DIM = 128
ROWS = 128
BLOCK = 256
CORE_HEADS = HEADS // 2
HALF = CORE_HEADS * HEAD_DIM
SCALE = HEAD_DIM**-0.5
EXP2_SCALE = SCALE * math.log2(math.e)
COST = pl.CostEstimate(flops=1, bytes_accessed=1, transcendentals=0)
CHUNKS = (3, 3, 3, 3)
PARITY = (0, 1, 0, 0)
ORDER = (
    "K0", "A3", "Q0", "A1", "A2", "A0", "B3", "B0", "D3", "B1",
    "B2", "D0", "E3", "D1", "E0", "D2", "F3", "E1", "R0", "E2",
    "G3", "F1", "F0", "F2", "S0", "G0", "H3", "G2", "H0", "G1",
    "T0", "H2", "H1",
)
VMEM_LIMIT = 40 * 2**20
EXTRACT_LIMIT = 62 * 2**20
BF16 = jnp.bfloat16
F32 = jnp.float32
ANYWHERE = pl.BlockSpec(memory_space=pl.ANY)


def params(steps=1):
    return pltpu.CompilerParams(
        dimension_semantics=("arbitrary",) * steps, vmem_limit_bytes=VMEM_LIMIT
    )


def averager(rows, group):
    row = lax.broadcasted_iota(jnp.int32, (rows, rows * group), 0)
    col = lax.broadcasted_iota(jnp.int32, (rows, rows * group), 1)
    return jnp.where(col // group == row, 1.0 / group, 0.0).astype(BF16)


def spreader(rows, group):
    row = lax.broadcasted_iota(jnp.int32, (rows * group, rows), 0)
    col = lax.broadcasted_iota(jnp.int32, (rows * group, rows), 1)
    return jnp.where(row // group == col, 1.0 / group, 0.0).astype(BF16)


def dot(a, b, dims=((1,), (0,))):
    return lax.dot_general(a, b, (dims, ((), ())), preferred_element_type=F32)


def extract_kernel(core, a_ref, b_ref, *refs):
    out_ref = refs[-1]
    out_ref[0] = a_ref[...]
    out_ref[1] = b_ref[...]


def extract_other(core, a, b, after, limit):
    half = pl.BlockSpec((ROWS, HALF), lambda i, c: (0, 1 - c[0]))
    return pl.pallas_call(
        extract_kernel,
        grid_spec=pltpu.PrefetchScalarGridSpec(
            num_scalar_prefetch=1,
            grid=(1,),
            in_specs=[half, half] + [ANYWHERE] * len(after),
            out_specs=pl.BlockSpec((2, ROWS, HALF), lambda i, c: (0, 0, 0)),
        ),
        out_shape=jax.ShapeDtypeStruct((2, ROWS, HALF), BF16),
        cost_estimate=COST,
        compiler_params=pltpu.CompilerParams(vmem_limit_bytes=limit),
        name="extract_other",
    )(core, a, b, *after)


def pack_first_kernel(core, k_ref, v_ref, kv_ref, *refs):
    first_out, own_out = refs[-2:]
    weights = jnp.concatenate(
        [averager(BLOCK >> level, 1 << level) for level in (1, 2, 3)], axis=0
    )
    for part, own in enumerate((k_ref, v_ref)):
        rows = jnp.concatenate([own[...], kv_ref[part]], axis=0)
        coarse = dot(weights, rows).astype(BF16)
        first_out[part] = coarse[:128]
        own_out[part] = coarse[128:]


def pack_first(core, start, heads, keys, values, kv_recv, after):
    own = pl.BlockSpec((ROWS, HEAD_DIM), lambda h, c: (0, c[0] * CORE_HEADS + start + h))
    recv = pl.BlockSpec((2, ROWS, HEAD_DIM), lambda h, c: (0, 0, start + h))
    return pl.pallas_call(
        pack_first_kernel,
        grid_spec=pltpu.PrefetchScalarGridSpec(
            num_scalar_prefetch=1,
            grid=(heads,),
            in_specs=[own, own, recv] + [ANYWHERE] * len(after),
            out_specs=[
                pl.BlockSpec((2, count, HEAD_DIM), lambda h, c: (0, 0, h)) for count in (128, 96)
            ],
        ),
        out_shape=[
            jax.ShapeDtypeStruct((2, count, heads * HEAD_DIM), BF16) for count in (128, 96)
        ],
        cost_estimate=COST,
        compiler_params=params(),
        name="pack_first",
    )(core, keys, values, kv_recv, *after)


def whole_call(kernel, name, out_shape, after, *args):
    return pl.pallas_call(
        kernel,
        in_specs=[pl.BlockSpec(memory_space=pltpu.VMEM)] * len(args) + [ANYWHERE] * len(after),
        out_specs=pl.BlockSpec(memory_space=pltpu.VMEM),
        out_shape=out_shape,
        cost_estimate=COST,
        compiler_params=pltpu.CompilerParams(vmem_limit_bytes=VMEM_LIMIT),
        name=name,
    )(*args, *after)


def pack_second_kernel(own_ref, first_ref, *refs):
    out_ref = refs[-1]
    pairs = averager(64, 2)
    for part in range(2):
        out_ref[part, :64] = own_ref[part, :64]
        out_ref[part, 64:] = dot(pairs, first_ref[part]).astype(BF16)


def pack_third_kernel(own_ref, first_ref, second_ref, *refs):
    out_ref = refs[-1]
    fours = averager(32, 4)
    pairs = averager(64, 2)
    for part in range(2):
        out_ref[part, :32] = own_ref[part, 64:]
        out_ref[part, 32:64] = dot(fours, first_ref[part]).astype(BF16)
        out_ref[part, 64:] = dot(pairs, second_ref[part]).astype(BF16)


def attend_kernel(
    core, q_own, g_own, k_own, v_own, qg_recv, kv_recv, first, second, third, *refs
):
    own_out, peer_out, exact_out, first_out, second_out, third_out = refs[-6:]
    queries = jnp.concatenate([q_own[...], qg_recv[0]], axis=0)
    grads = jnp.concatenate([g_own[...], qg_recv[1]], axis=0)
    keys = jnp.concatenate([k_own[...], kv_recv[0], first[0], second[0], third[0]], axis=0)
    values = jnp.concatenate([v_own[...], kv_recv[1], first[1], second[1], third[1]], axis=0)
    scores = dot(keys, queries, ((1,), (1,)))
    row_max = jnp.max(scores, axis=0, keepdims=True)
    exp_scores = jnp.exp2((scores - row_max) * EXP2_SCALE)
    weights = exp_scores * (1.0 / jnp.sum(exp_scores, axis=0, keepdims=True))
    weights_low = weights.astype(BF16)
    prob_grad = dot(values, grads, ((1,), (1,)))
    row_inner = jnp.sum(weights * prob_grad, axis=0, keepdims=True)
    score_grad = (weights * (prob_grad - row_inner)).astype(BF16)
    attended = dot(values.T, weights_low).T
    query_grad = dot(keys.T, score_grad).T * SCALE
    for part, result in enumerate((attended, query_grad)):
        result = result.astype(BF16)
        own_out[part] = result[:ROWS]
        peer_out[part] = result[ROWS:]
    key_terms = dot(score_grad, queries) * SCALE
    value_terms = dot(weights_low, grads)
    for part, terms in enumerate((key_terms, value_terms)):
        exact_out[part] = terms[:256]
        first_out[part] = terms[256:384]
        second_out[part] = terms[384:512]
        third_out[part] = terms[512:].astype(BF16)


def attend(core, start, heads, q, g, k, v, qg_recv, kv_recv, first, second, third, chain, after):
    own = pl.BlockSpec((ROWS, HEAD_DIM), lambda h, c: (0, c[0] * CORE_HEADS + start + h))
    recv = pl.BlockSpec((2, ROWS, HEAD_DIM), lambda h, c: (0, 0, start + h))
    local = pl.BlockSpec((2, ROWS, HEAD_DIM), lambda h, c: (0, 0, h))
    local_exact = pl.BlockSpec((2, BLOCK, HEAD_DIM), lambda h, c: (0, 0, h))
    width = heads * HEAD_DIM
    ops = 6 * 2 * 256 * 640 * 128 * heads
    chain = list(chain) if chain is not None else []
    return pl.pallas_call(
        attend_kernel,
        grid_spec=pltpu.PrefetchScalarGridSpec(
            num_scalar_prefetch=1,
            grid=(heads,),
            in_specs=[own] * 4 + [recv] * 2 + [local] * 3 + [ANYWHERE] * (len(chain) + len(after)),
            out_specs=[recv, recv, local_exact, local, local, local],
        ),
        out_shape=[
            jax.ShapeDtypeStruct((2, ROWS, HALF), BF16),
            jax.ShapeDtypeStruct((2, ROWS, HALF), BF16),
            jax.ShapeDtypeStruct((2, BLOCK, width), F32),
            jax.ShapeDtypeStruct((2, ROWS, width), F32),
            jax.ShapeDtypeStruct((2, ROWS, width), F32),
            jax.ShapeDtypeStruct((2, ROWS, width), BF16),
        ],
        input_output_aliases={10: 0, 11: 1} if chain else {},
        cost_estimate=COST,
        compiler_params=params(),
        name="attend",
    )(core, q, g, k, v, qg_recv, kv_recv, first, second, third, *chain, *after)


def back_second_kernel(second_ref, third_ref, *refs):
    out_ref = refs[-1]
    pairs = spreader(64, 2)
    for part in range(2):
        out_ref[part] = (second_ref[part] + dot(pairs, third_ref[part, 64:])).astype(BF16)


def back_first_kernel(first_ref, second_ref, third_ref, *refs):
    out_ref = refs[-1]
    pairs = spreader(64, 2)
    fours = spreader(32, 4)
    for part in range(2):
        out_ref[part] = (
            first_ref[part]
            + dot(pairs, second_ref[part, 64:])
            + dot(fours, third_ref[part, 32:64])
        ).astype(BF16)


def finish_kernel(exact_ref, first_ref, second_ref, third_ref, *refs):
    own_out, peer_out, token = refs[-3:]
    token[...] = jnp.zeros_like(token)
    for part in range(2):
        total = (
            exact_ref[part]
            + dot(spreader(128, 2), first_ref[part])
            + dot(spreader(64, 4), second_ref[part, :64])
            + dot(spreader(32, 8), third_ref[part, :32])
        ).astype(BF16)
        own_out[part] = total[:ROWS]
        peer_out[part] = total[ROWS:]


def finish(start, heads, exact, first, second, third, chain, after):
    local = pl.BlockSpec((2, ROWS, HEAD_DIM), lambda h: (0, 0, h))
    local_exact = pl.BlockSpec((2, BLOCK, HEAD_DIM), lambda h: (0, 0, h))
    placed = pl.BlockSpec((2, ROWS, HEAD_DIM), lambda h: (0, 0, start + h))
    chain = list(chain) if chain is not None else []
    return pl.pallas_call(
        finish_kernel,
        grid=(heads,),
        in_specs=[local_exact, local, local, local] + [ANYWHERE] * (len(chain) + len(after)),
        out_specs=[placed, placed, pl.BlockSpec((8, 128), lambda h: (0, 0))],
        out_shape=[jax.ShapeDtypeStruct((2, ROWS, HALF), BF16)] * 2
        + [jax.ShapeDtypeStruct((8, 128), F32)],
        input_output_aliases={4: 0, 5: 1} if chain else {},
        cost_estimate=COST,
        compiler_params=params(),
        name="finish",
    )(exact, first, second, third, *chain, *after)


def assemble_kernel(core, own_ref, recv_ref, *refs):
    a_ref, b_ref, token = refs[-3:]
    token[...] = jnp.zeros_like(token)
    mine = pl.program_id(0) == core[0]

    @pl.when(mine)
    def _():
        a_ref[...] = own_ref[0]
        b_ref[...] = own_ref[1]

    @pl.when(jnp.logical_not(mine))
    def _():
        a_ref[...] = recv_ref[0]
        b_ref[...] = recv_ref[1]


def assemble(core, own, recv, after):
    whole = pl.BlockSpec((2, ROWS, HALF), lambda j, c: (0, 0, 0))
    half = pl.BlockSpec((ROWS, HALF), lambda j, c: (0, j))
    return pl.pallas_call(
        assemble_kernel,
        grid_spec=pltpu.PrefetchScalarGridSpec(
            num_scalar_prefetch=1, grid=(2,), in_specs=[whole, whole] + [ANYWHERE] * len(after),
            out_specs=[half, half, pl.BlockSpec((8, 128), lambda j, c: (0, 0))],
        ),
        out_shape=[jax.ShapeDtypeStruct((ROWS, 2 * HALF), BF16)] * 2
        + [jax.ShapeDtypeStruct((8, 128), F32)],
        cost_estimate=COST,
        compiler_params=params(),
        name="assemble",
    )(core, own, recv, *after)


def swap_core(block):
    return lax.ppermute(block, "fine", [(i, i ^ 1) for i in range(lax.axis_size("fine"))])


def swap_fine(block, mask):
    return lax.ppermute(block, "fine", [(i, i ^ mask) for i in range(lax.axis_size("fine"))])


def swap_next(block, odd):
    fine, coarse = lax.axis_size("fine"), lax.axis_size("coarse")
    route = []
    for f in range(fine):
        for c in range(coarse):
            z = (f // 2) * 2 + c % 2
            if odd:
                there = (z + 1 if z % 2 else z - 1) % fine
            else:
                there = z ^ 1
            route.append((f * coarse + c, (there // 2 * 2 + f % 2) * coarse + c - c % 2 + there % 2))
    return lax.ppermute(block, ("fine", "coarse"), route)


def body(query_rows, key_rows, value_rows, out_grad):
    full_shape = query_rows.shape
    queries, keys, values, grads = (
        block.reshape(ROWS, 2 * HALF) for block in (query_rows, key_rows, value_rows, out_grad)
    )
    core = (lax.axis_index("fine") % 2).astype(jnp.int32).reshape(1)
    count = len(CHUNKS)
    starts = [sum(CHUNKS[:n]) for n in range(count)]
    own_packed, first, second, third = ([None] * count for _ in range(4))
    results, third_back, second_back, first_back = ([None] * count for _ in range(4))
    a_chain, b_chain, a_recv, after = None, None, None, []

    def shape_of(n):
        return jax.ShapeDtypeStruct((2, ROWS, CHUNKS[n] * HEAD_DIM), BF16)

    for step in ORDER:
        kind, n = step[0], int(step[1:])
        if kind == "K":
            send = extract_other(core, keys, values, after, EXTRACT_LIMIT)
            kv_recv = swap_core(send)
        elif kind == "Q":
            send = extract_other(core, queries, grads, after, VMEM_LIMIT)
            qg_recv = swap_core(send)
        elif kind == "A":
            send, own_packed[n] = pack_first(core, starts[n], CHUNKS[n], keys, values, kv_recv, after)
            first[n] = swap_fine(send, 2)
        elif kind == "B":
            send = whole_call(
                pack_second_kernel, "pack_second", shape_of(n), after, own_packed[n], first[n]
            )
            second[n] = swap_fine(send, 6)
        elif kind == "D":
            send = whole_call(
                pack_third_kernel, "pack_third", shape_of(n), after, own_packed[n], first[n], second[n]
            )
            third[n] = swap_next(send, PARITY[n])
        elif kind == "E":
            results[n] = attend(
                core, starts[n], CHUNKS[n], queries, grads, keys, values, qg_recv, kv_recv,
                first[n], second[n], third[n], a_chain, after,
            )
            a_chain = results[n][:2]
            send = results[n][5]
            third_back[n] = swap_next(send, PARITY[n])
        elif kind == "F":
            send = whole_call(
                back_second_kernel, "back_second", shape_of(n), after, results[n][4], third_back[n]
            )
            second_back[n] = swap_fine(send, 6)
        elif kind == "G":
            send = whole_call(
                back_first_kernel, "back_first", shape_of(n), after,
                results[n][3], second_back[n], third_back[n],
            )
            first_back[n] = swap_fine(send, 2)
        elif kind == "H":
            *b_chain, send = finish(
                starts[n], CHUNKS[n], results[n][2], first_back[n], second_back[n], third_back[n],
                b_chain, after,
            )
        elif kind == "S":
            a_recv = swap_core(a_chain[1])
            continue
        elif kind == "R":
            after = after + [qg_recv]
            continue
        elif kind == "T":
            attended, query_grad, send = assemble(core, a_chain[0], a_recv, after)
        after = [send]
    b_recv = swap_core(b_chain[1])
    key_grad, value_grad, _ = assemble(core, b_chain[0], b_recv, after)
    return tuple(
        block.reshape(full_shape) for block in (attended, query_grad, key_grad, value_grad)
    )


def solution(mesh):
    placed = P("coarse", "fine", None, None)
    return jax.shard_map(
        body, mesh=mesh, in_specs=(placed,) * 4, out_specs=(placed,) * 4, check_vma=False
    )
```

```python
import functools
import math

import jax
import jax.numpy as jnp
from jax import lax
from jax.experimental import pallas as pl
from jax.experimental.pallas import tpu as pltpu
from jax.sharding import PartitionSpec as P

HEADS = 24
HEAD_DIM = 128
ROWS = 128
BLOCK = 256
CORE_HEADS = HEADS // 2
HALF = CORE_HEADS * HEAD_DIM
SCALE = HEAD_DIM**-0.5
EXP2_SCALE = SCALE * math.log2(math.e)
COST = pl.CostEstimate(flops=1, bytes_accessed=1, transcendentals=0)
CHUNKS = (3, 3, 3, 3)
PARITY = (0, 0, 0, 1)
ORDER = (
    "K0", "Q0", "A0", "B1", "B2", "D1", "B3", "B0", "D2", "E1",
    "D3", "E2", "D0", "F1", "E3", "E0", "G1", "S0", "F3", "R0",
    "F2", "F0", "G2", "H1", "G0", "H2", "G3", "H0", "T0", "H3",
)
VMEM_LIMIT = 40 * 2**20
BF16 = jnp.bfloat16
F32 = jnp.float32
ANYWHERE = pl.BlockSpec(memory_space=pl.ANY)


def params(steps=1):
    return pltpu.CompilerParams(
        dimension_semantics=("arbitrary",) * steps, vmem_limit_bytes=VMEM_LIMIT
    )


def averager(rows, group):
    row = lax.broadcasted_iota(jnp.int32, (rows, rows * group), 0)
    col = lax.broadcasted_iota(jnp.int32, (rows, rows * group), 1)
    return jnp.where(col // group == row, 1.0 / group, 0.0).astype(BF16)


def spreader(rows, group):
    row = lax.broadcasted_iota(jnp.int32, (rows * group, rows), 0)
    col = lax.broadcasted_iota(jnp.int32, (rows * group, rows), 1)
    return jnp.where(row // group == col, 1.0 / group, 0.0).astype(BF16)


def dot(a, b, dims=((1,), (0,))):
    return lax.dot_general(a, b, (dims, ((), ())), preferred_element_type=F32)


def extract_kernel(core, a_ref, b_ref, *refs):
    out_ref = refs[-1]
    out_ref[0] = a_ref[...]
    out_ref[1] = b_ref[...]


def extract_other(core, a, b, after, limit):
    half = pl.BlockSpec((ROWS, HALF), lambda i, c: (0, 1 - c[0]))
    return pl.pallas_call(
        extract_kernel,
        grid_spec=pltpu.PrefetchScalarGridSpec(
            num_scalar_prefetch=1,
            grid=(1,),
            in_specs=[half, half] + [ANYWHERE] * len(after),
            out_specs=pl.BlockSpec((2, ROWS, HALF), lambda i, c: (0, 0, 0)),
        ),
        out_shape=jax.ShapeDtypeStruct((2, ROWS, HALF), BF16),
        cost_estimate=COST,
        compiler_params=pltpu.CompilerParams(vmem_limit_bytes=limit),
        name="extract_other",
    )(core, a, b, *after)


def pack_first_kernel(core, k_ref, v_ref, kv_ref, *refs):
    outs = refs[-2 * len(CHUNKS) :]
    weights = jnp.concatenate(
        [averager(BLOCK >> level, 1 << level) for level in (1, 2, 3)], axis=0
    )
    for part, own in enumerate((k_ref, v_ref)):
        rows = jnp.concatenate([own[...], kv_ref[part]], axis=0)
        lane = 0
        for number, heads in enumerate(CHUNKS):
            width = heads * HEAD_DIM
            coarse = dot(weights, rows[:, lane : lane + width]).astype(BF16)
            outs[2 * number][part] = coarse[:128]
            outs[2 * number + 1][part] = coarse[128:]
            lane += width


def pack_first(core, keys, values, kv_recv, after):
    half = pl.BlockSpec((ROWS, HALF), lambda i, c: (0, c[0]))
    whole = pl.BlockSpec((2, ROWS, HALF), lambda i, c: (0, 0, 0))
    shapes = [(2, count, heads * HEAD_DIM) for heads in CHUNKS for count in (128, 96)]
    return pl.pallas_call(
        pack_first_kernel,
        grid_spec=pltpu.PrefetchScalarGridSpec(
            num_scalar_prefetch=1,
            grid=(1,),
            in_specs=[half, half, whole] + [ANYWHERE] * len(after),
            out_specs=[pl.BlockSpec(shape, lambda i, c: (0, 0, 0)) for shape in shapes],
        ),
        out_shape=[jax.ShapeDtypeStruct(shape, BF16) for shape in shapes],
        cost_estimate=COST,
        compiler_params=params(),
        name="pack_first",
    )(core, keys, values, kv_recv, *after)


def whole_call(kernel, name, out_shape, after, *args):
    return pl.pallas_call(
        kernel,
        in_specs=[pl.BlockSpec(memory_space=pltpu.VMEM)] * len(args) + [ANYWHERE] * len(after),
        out_specs=pl.BlockSpec(memory_space=pltpu.VMEM),
        out_shape=out_shape,
        cost_estimate=COST,
        compiler_params=pltpu.CompilerParams(vmem_limit_bytes=VMEM_LIMIT),
        name=name,
    )(*args, *after)


def pack_second_kernel(own_ref, first_ref, *refs):
    out_ref = refs[-1]
    pairs = averager(64, 2)
    for part in range(2):
        out_ref[part, :64] = own_ref[part, :64]
        out_ref[part, 64:] = dot(pairs, first_ref[part]).astype(BF16)


def pack_third_kernel(own_ref, first_ref, second_ref, *refs):
    out_ref = refs[-1]
    fours = averager(32, 4)
    pairs = averager(64, 2)
    for part in range(2):
        out_ref[part, :32] = own_ref[part, 64:]
        out_ref[part, 32:64] = dot(fours, first_ref[part]).astype(BF16)
        out_ref[part, 64:] = dot(pairs, second_ref[part]).astype(BF16)


def attend_kernel(
    core, q_own, g_own, k_own, v_own, qg_recv, kv_recv, first, second, third, *refs
):
    own_out, peer_out, exact_out, first_out, second_out, third_out = refs[-6:]
    queries = jnp.concatenate([q_own[...], qg_recv[0]], axis=0)
    grads = jnp.concatenate([g_own[...], qg_recv[1]], axis=0)
    keys = jnp.concatenate([k_own[...], kv_recv[0], first[0], second[0], third[0]], axis=0)
    values = jnp.concatenate([v_own[...], kv_recv[1], first[1], second[1], third[1]], axis=0)
    scores = dot(keys, queries, ((1,), (1,)))
    row_max = jnp.max(scores, axis=0, keepdims=True)
    exp_scores = jnp.exp2((scores - row_max) * EXP2_SCALE)
    weights = exp_scores * (1.0 / jnp.sum(exp_scores, axis=0, keepdims=True))
    weights_low = weights.astype(BF16)
    prob_grad = dot(values, grads, ((1,), (1,)))
    row_inner = jnp.sum(weights * prob_grad, axis=0, keepdims=True)
    score_grad = (weights * (prob_grad - row_inner)).astype(BF16)
    attended = dot(values.T, weights_low).T
    query_grad = dot(keys.T, score_grad).T * SCALE
    for part, result in enumerate((attended, query_grad)):
        result = result.astype(BF16)
        own_out[part] = result[:ROWS]
        peer_out[part] = result[ROWS:]
    key_terms = dot(score_grad, queries) * SCALE
    value_terms = dot(weights_low, grads)
    for part, terms in enumerate((key_terms, value_terms)):
        exact_out[part] = terms[:256]
        first_out[part] = terms[256:384]
        second_out[part] = terms[384:512]
        third_out[part] = terms[512:].astype(BF16)


def attend(core, start, heads, q, g, k, v, qg_recv, kv_recv, first, second, third, chain, after):
    own = pl.BlockSpec((ROWS, HEAD_DIM), lambda h, c: (0, c[0] * CORE_HEADS + start + h))
    recv = pl.BlockSpec((2, ROWS, HEAD_DIM), lambda h, c: (0, 0, start + h))
    local = pl.BlockSpec((2, ROWS, HEAD_DIM), lambda h, c: (0, 0, h))
    local_exact = pl.BlockSpec((2, BLOCK, HEAD_DIM), lambda h, c: (0, 0, h))
    width = heads * HEAD_DIM
    ops = 6 * 2 * 256 * 640 * 128 * heads
    chain = list(chain) if chain is not None else []
    return pl.pallas_call(
        attend_kernel,
        grid_spec=pltpu.PrefetchScalarGridSpec(
            num_scalar_prefetch=1,
            grid=(heads,),
            in_specs=[own] * 4 + [recv] * 2 + [local] * 3 + [ANYWHERE] * (len(chain) + len(after)),
            out_specs=[recv, recv, local_exact, local, local, local],
        ),
        out_shape=[
            jax.ShapeDtypeStruct((2, ROWS, HALF), BF16),
            jax.ShapeDtypeStruct((2, ROWS, HALF), BF16),
            jax.ShapeDtypeStruct((2, BLOCK, width), F32),
            jax.ShapeDtypeStruct((2, ROWS, width), F32),
            jax.ShapeDtypeStruct((2, ROWS, width), F32),
            jax.ShapeDtypeStruct((2, ROWS, width), BF16),
        ],
        input_output_aliases={10: 0, 11: 1} if chain else {},
        cost_estimate=COST,
        compiler_params=params(),
        name="attend",
    )(core, q, g, k, v, qg_recv, kv_recv, first, second, third, *chain, *after)


def back_second_kernel(second_ref, third_ref, *refs):
    out_ref = refs[-1]
    pairs = spreader(64, 2)
    for part in range(2):
        out_ref[part] = (second_ref[part] + dot(pairs, third_ref[part, 64:])).astype(BF16)


def back_first_kernel(first_ref, second_ref, third_ref, *refs):
    out_ref = refs[-1]
    pairs = spreader(64, 2)
    fours = spreader(32, 4)
    for part in range(2):
        out_ref[part] = (
            first_ref[part]
            + dot(pairs, second_ref[part, 64:])
            + dot(fours, third_ref[part, 32:64])
        ).astype(BF16)


def finish_kernel(start, heads, exact_ref, first_ref, second_ref, third_ref, *refs):
    own_out, peer_out, token, total_ref, sems = refs[-5:]
    token[...] = jnp.zeros_like(token)
    weights = jnp.concatenate(
        [spreader(128, 2), spreader(64, 4), spreader(32, 8)], axis=1
    )
    for part in range(2):
        rows = jnp.concatenate(
            [first_ref[part], second_ref[part, :64], third_ref[part, :32]], axis=0
        )
        total_ref[part] = (exact_ref[part] + dot(weights, rows)).astype(BF16)
    lanes = pl.ds(start * HEAD_DIM, heads * HEAD_DIM)
    copies = [
        pltpu.make_async_copy(
            total_ref.at[:, pl.ds(part * ROWS, ROWS)], out.at[:, :, lanes], sems.at[part]
        )
        for part, out in enumerate((own_out, peer_out))
    ]
    for copy in copies:
        copy.start()
    for copy in copies:
        copy.wait()


def finish(start, heads, exact, first, second, third, chain, after):
    in_vmem = pl.BlockSpec(memory_space=pltpu.VMEM)
    chain = list(chain) if chain is not None else []
    return pl.pallas_call(
        functools.partial(finish_kernel, start, heads),
        in_specs=[in_vmem] * 4 + [ANYWHERE] * (len(chain) + len(after)),
        out_specs=[ANYWHERE, ANYWHERE, in_vmem],
        out_shape=[jax.ShapeDtypeStruct((2, ROWS, HALF), BF16)] * 2
        + [jax.ShapeDtypeStruct((8, 128), F32)],
        scratch_shapes=[
            pltpu.VMEM((2, BLOCK, heads * HEAD_DIM), BF16),
            pltpu.SemaphoreType.DMA((2,)),
        ],
        input_output_aliases={4: 0, 5: 1} if chain else {},
        cost_estimate=COST,
        compiler_params=pltpu.CompilerParams(vmem_limit_bytes=VMEM_LIMIT),
        name="finish",
    )(exact, first, second, third, *chain, *after)


def assemble_kernel(core, own_ref, recv_ref, *refs):
    a_ref, b_ref, token = refs[-3:]
    token[...] = jnp.zeros_like(token)
    mine = pl.program_id(0) == core[0]

    @pl.when(mine)
    def _():
        a_ref[...] = own_ref[0]
        b_ref[...] = own_ref[1]

    @pl.when(jnp.logical_not(mine))
    def _():
        a_ref[...] = recv_ref[0]
        b_ref[...] = recv_ref[1]


def assemble(core, own, recv, after):
    whole = pl.BlockSpec((2, ROWS, HALF), lambda j, c: (0, 0, 0))
    half = pl.BlockSpec((ROWS, HALF), lambda j, c: (0, j))
    return pl.pallas_call(
        assemble_kernel,
        grid_spec=pltpu.PrefetchScalarGridSpec(
            num_scalar_prefetch=1, grid=(2,), in_specs=[whole, whole] + [ANYWHERE] * len(after),
            out_specs=[half, half, pl.BlockSpec((8, 128), lambda j, c: (0, 0))],
        ),
        out_shape=[jax.ShapeDtypeStruct((ROWS, 2 * HALF), BF16)] * 2
        + [jax.ShapeDtypeStruct((8, 128), F32)],
        cost_estimate=COST,
        compiler_params=params(),
        name="assemble",
    )(core, own, recv, *after)


def swap_core(block):
    return lax.ppermute(block, "fine", [(i, i ^ 1) for i in range(lax.axis_size("fine"))])


def swap_fine(block, mask):
    return lax.ppermute(block, "fine", [(i, i ^ mask) for i in range(lax.axis_size("fine"))])


def swap_next(block, odd):
    fine, coarse = lax.axis_size("fine"), lax.axis_size("coarse")
    route = []
    for f in range(fine):
        for c in range(coarse):
            z = (f // 2) * 2 + c % 2
            if odd:
                there = (z + 1 if z % 2 else z - 1) % fine
            else:
                there = z ^ 1
            route.append((f * coarse + c, (there // 2 * 2 + f % 2) * coarse + c - c % 2 + there % 2))
    return lax.ppermute(block, ("fine", "coarse"), route)


def body(query_rows, key_rows, value_rows, out_grad):
    full_shape = query_rows.shape
    queries, keys, values, grads = (
        block.reshape(ROWS, 2 * HALF) for block in (query_rows, key_rows, value_rows, out_grad)
    )
    core = (lax.axis_index("fine") % 2).astype(jnp.int32).reshape(1)
    count = len(CHUNKS)
    starts = [sum(CHUNKS[:n]) for n in range(count)]
    own_packed, first, second, third = ([None] * count for _ in range(4))
    results, third_back, second_back, first_back = ([None] * count for _ in range(4))
    a_chain, b_chain, a_recv, after = None, None, None, []

    def shape_of(n):
        return jax.ShapeDtypeStruct((2, ROWS, CHUNKS[n] * HEAD_DIM), BF16)

    for step in ORDER:
        kind, n = step[0], int(step[1:])
        if kind == "K":
            send = extract_other(core, keys, values, after, VMEM_LIMIT)
            kv_recv = swap_core(send)
        elif kind == "Q":
            send = extract_other(core, queries, grads, after, VMEM_LIMIT)
            qg_recv = swap_core(send)
        elif kind == "A":
            packed = pack_first(core, keys, values, kv_recv, after)
            own_packed = packed[1::2]
            first = [swap_fine(rows, 2) for rows in packed[::2]]
            send = packed[0]
        elif kind == "B":
            send = whole_call(
                pack_second_kernel, "pack_second", shape_of(n), after, own_packed[n], first[n]
            )
            second[n] = swap_fine(send, 6)
        elif kind == "D":
            send = whole_call(
                pack_third_kernel, "pack_third", shape_of(n), after, own_packed[n], first[n], second[n]
            )
            third[n] = swap_next(send, PARITY[n])
        elif kind == "E":
            results[n] = attend(
                core, starts[n], CHUNKS[n], queries, grads, keys, values, qg_recv, kv_recv,
                first[n], second[n], third[n], a_chain, after,
            )
            a_chain = results[n][:2]
            send = results[n][5]
            third_back[n] = swap_next(send, PARITY[n])
        elif kind == "F":
            send = whole_call(
                back_second_kernel, "back_second", shape_of(n), after, results[n][4], third_back[n]
            )
            second_back[n] = swap_fine(send, 6)
        elif kind == "G":
            send = whole_call(
                back_first_kernel, "back_first", shape_of(n), after,
                results[n][3], second_back[n], third_back[n],
            )
            first_back[n] = swap_fine(send, 2)
        elif kind == "H":
            *b_chain, send = finish(
                starts[n], CHUNKS[n], results[n][2], first_back[n], second_back[n], third_back[n],
                b_chain, after,
            )
        elif kind == "S":
            a_recv = swap_core(a_chain[1])
            continue
        elif kind == "R":
            after = after + [qg_recv]
            continue
        elif kind == "T":
            attended, query_grad, send = assemble(core, a_chain[0], a_recv, after)
        after = [send]
    b_recv = swap_core(b_chain[1])
    key_grad, value_grad, _ = assemble(core, b_chain[0], b_recv, after)
    return tuple(
        block.reshape(full_shape) for block in (attended, query_grad, key_grad, value_grad)
    )


def solution(mesh):
    placed = P("coarse", "fine", None, None)
    return jax.shard_map(
        body, mesh=mesh, in_specs=(placed,) * 4, out_specs=(placed,) * 4, check_vma=False
    )
```

```python
import functools
import math

import jax
import jax.numpy as jnp
from jax import lax
from jax.experimental import pallas as pl
from jax.experimental.pallas import tpu as pltpu
from jax.sharding import PartitionSpec as P

HEADS = 24
HEAD_DIM = 128
ROWS = 128
BLOCK = 256
CORE_HEADS = HEADS // 2
HALF = CORE_HEADS * HEAD_DIM
SCALE = HEAD_DIM**-0.5
EXP2_SCALE = SCALE * math.log2(math.e)
COST = pl.CostEstimate(flops=1, bytes_accessed=1, transcendentals=0)
CHUNKS = (3, 3, 3, 3)
PARITY = (0, 0, 0, 1)
ORDER = (
    "K0", "Q0", "A0", "B1", "B2", "D1", "B3", "B0", "D2", "E1",
    "D3", "E2", "D0", "F1", "E3", "E0", "G1", "S0", "F3", "R0",
    "F2", "F0", "G2", "H1", "G0", "H2", "G3", "H0", "T0", "H3",
)
VMEM_LIMIT = 40 * 2**20
BF16 = jnp.bfloat16
F32 = jnp.float32
ANYWHERE = pl.BlockSpec(memory_space=pl.ANY)


def params(steps=1):
    return pltpu.CompilerParams(
        dimension_semantics=("arbitrary",) * steps, vmem_limit_bytes=VMEM_LIMIT
    )


def averager(rows, group):
    row = lax.broadcasted_iota(jnp.int32, (rows, rows * group), 0)
    col = lax.broadcasted_iota(jnp.int32, (rows, rows * group), 1)
    return jnp.where(col // group == row, 1.0 / group, 0.0).astype(BF16)


def spreader(rows, group):
    row = lax.broadcasted_iota(jnp.int32, (rows * group, rows), 0)
    col = lax.broadcasted_iota(jnp.int32, (rows * group, rows), 1)
    return jnp.where(row // group == col, 1.0 / group, 0.0).astype(BF16)


def dot(a, b, dims=((1,), (0,))):
    return lax.dot_general(a, b, (dims, ((), ())), preferred_element_type=F32)


def extract_kernel(core, a_ref, b_ref, *refs):
    out_ref = refs[-1]
    out_ref[0] = a_ref[...]
    out_ref[1] = b_ref[...]


def extract_other(core, a, b, after, limit):
    half = pl.BlockSpec((ROWS, HALF), lambda i, c: (0, 1 - c[0]))
    return pl.pallas_call(
        extract_kernel,
        grid_spec=pltpu.PrefetchScalarGridSpec(
            num_scalar_prefetch=1,
            grid=(1,),
            in_specs=[half, half] + [ANYWHERE] * len(after),
            out_specs=pl.BlockSpec((2, ROWS, HALF), lambda i, c: (0, 0, 0)),
        ),
        out_shape=jax.ShapeDtypeStruct((2, ROWS, HALF), BF16),
        cost_estimate=COST,
        compiler_params=pltpu.CompilerParams(vmem_limit_bytes=limit),
        name="extract_other",
    )(core, a, b, *after)


def pack_first_kernel(core, k_ref, v_ref, kv_ref, *refs):
    outs = refs[-2 * len(CHUNKS) :]
    weights = jnp.concatenate(
        [averager(BLOCK >> level, 1 << level) for level in (1, 2, 3)], axis=0
    )
    for part, own in enumerate((k_ref, v_ref)):
        rows = jnp.concatenate([own[...], kv_ref[part]], axis=0)
        lane = 0
        for number, heads in enumerate(CHUNKS):
            width = heads * HEAD_DIM
            coarse = dot(weights, rows[:, lane : lane + width]).astype(BF16)
            outs[2 * number][part] = coarse[:128]
            outs[2 * number + 1][part] = coarse[128:]
            lane += width


def pack_first(core, keys, values, kv_recv, after):
    half = pl.BlockSpec((ROWS, HALF), lambda i, c: (0, c[0]))
    whole = pl.BlockSpec((2, ROWS, HALF), lambda i, c: (0, 0, 0))
    shapes = [(2, count, heads * HEAD_DIM) for heads in CHUNKS for count in (128, 96)]
    return pl.pallas_call(
        pack_first_kernel,
        grid_spec=pltpu.PrefetchScalarGridSpec(
            num_scalar_prefetch=1,
            grid=(1,),
            in_specs=[half, half, whole] + [ANYWHERE] * len(after),
            out_specs=[pl.BlockSpec(shape, lambda i, c: (0, 0, 0)) for shape in shapes],
        ),
        out_shape=[jax.ShapeDtypeStruct(shape, BF16) for shape in shapes],
        cost_estimate=COST,
        compiler_params=params(),
        name="pack_first",
    )(core, keys, values, kv_recv, *after)


def whole_call(kernel, name, out_shape, after, *args):
    return pl.pallas_call(
        kernel,
        in_specs=[pl.BlockSpec(memory_space=pltpu.VMEM)] * len(args) + [ANYWHERE] * len(after),
        out_specs=pl.BlockSpec(memory_space=pltpu.VMEM),
        out_shape=out_shape,
        cost_estimate=COST,
        compiler_params=pltpu.CompilerParams(vmem_limit_bytes=VMEM_LIMIT),
        name=name,
    )(*args, *after)


def pack_second_kernel(own_ref, first_ref, *refs):
    out_ref = refs[-1]
    pairs = averager(64, 2)
    for part in range(2):
        out_ref[part, :64] = own_ref[part, :64]
        out_ref[part, 64:] = dot(pairs, first_ref[part]).astype(BF16)


def pack_third_kernel(own_ref, first_ref, second_ref, *refs):
    out_ref = refs[-1]
    fours = averager(32, 4)
    pairs = averager(64, 2)
    for part in range(2):
        out_ref[part, :32] = own_ref[part, 64:]
        out_ref[part, 32:64] = dot(fours, first_ref[part]).astype(BF16)
        out_ref[part, 64:] = dot(pairs, second_ref[part]).astype(BF16)


def attend_kernel(start, heads, core, q_own, g_own, k_own, v_own, *refs):
    for head in range(heads):
        attend_head(start, head, core, q_own, g_own, k_own, v_own, *refs)


def attend_head(
    start, head, core, q_own, g_own, k_own, v_own, qg_recv, kv_recv, first, second, third, *refs
):
    own_out, peer_out, exact_out, first_out, second_out, third_out = refs[-6:]
    own = pl.ds(pl.multiple_of(core[0] * HALF + (start + head) * HEAD_DIM, HEAD_DIM), HEAD_DIM)
    recv = pl.ds((start + head) * HEAD_DIM, HEAD_DIM)
    local = pl.ds(head * HEAD_DIM, HEAD_DIM)
    queries = jnp.concatenate([q_own[:, own], qg_recv[0, :, recv]], axis=0)
    grads = jnp.concatenate([g_own[:, own], qg_recv[1, :, recv]], axis=0)
    keys, values = (
        jnp.concatenate(
            [mine[:, own], kv_recv[part, :, recv]]
            + [rows[part, :, local] for rows in (first, second, third)],
            axis=0,
        )
        for part, mine in enumerate((k_own, v_own))
    )
    scores = dot(keys, queries, ((1,), (1,)))
    prob_grad = dot(values, grads, ((1,), (1,)))
    pieces = [slice(low, low + ROWS) for low in range(0, 5 * ROWS, ROWS)]

    def fold(block):
        return block.reshape(ROWS // 8, 8, BLOCK)

    tops = [jnp.max(fold(scores[piece]), axis=0) for piece in pieces]
    row_max = jnp.max(functools.reduce(jnp.maximum, tops), axis=0, keepdims=True)
    exp_scores, exp_sum, exp_grad = [], 0.0, 0.0
    for piece in pieces:
        block = jnp.exp2((scores[piece] - row_max) * EXP2_SCALE)
        exp_scores.append(block)
        exp_sum += jnp.sum(fold(block), axis=0)
        exp_grad += jnp.sum(fold(block * prob_grad[piece]), axis=0)
    inverse = 1.0 / jnp.sum(exp_sum, axis=0, keepdims=True)
    row_inner = jnp.sum(exp_grad, axis=0, keepdims=True) * inverse
    weights_low, score_grad = [], []
    for piece, block in zip(pieces, exp_scores):
        weights = block * inverse
        weights_low.append(weights.astype(BF16))
        score_grad.append((weights * (prob_grad[piece] - row_inner)).astype(BF16))
    weights_low = jnp.concatenate(weights_low, axis=0)
    score_grad = jnp.concatenate(score_grad, axis=0)
    attended = dot(values.T, weights_low).T
    query_grad = dot(keys.T, score_grad).T * SCALE
    for part, result in enumerate((attended, query_grad)):
        result = result.astype(BF16)
        own_out[part, :, recv] = result[:ROWS]
        peer_out[part, :, recv] = result[ROWS:]
    key_terms = dot(score_grad, queries) * SCALE
    value_terms = dot(weights_low, grads)
    for part, terms in enumerate((key_terms, value_terms)):
        exact_out[part, :, local] = terms[:256]
        first_out[part, :, local] = terms[256:384]
        second_out[part, :, local] = terms[384:512]
        third_out[part, :, local] = terms[512:].astype(BF16)


def attend(core, start, heads, q, g, k, v, qg_recv, kv_recv, first, second, third, chain, after):
    in_vmem = pl.BlockSpec(memory_space=pltpu.VMEM)
    width = heads * HEAD_DIM
    chain = list(chain) if chain is not None else []
    return pl.pallas_call(
        functools.partial(attend_kernel, start, heads),
        in_specs=[pl.BlockSpec(memory_space=pltpu.SMEM)]
        + [in_vmem] * (9 + len(chain))
        + [ANYWHERE] * len(after),
        out_specs=[in_vmem] * 6,
        out_shape=[
            jax.ShapeDtypeStruct((2, ROWS, HALF), BF16),
            jax.ShapeDtypeStruct((2, ROWS, HALF), BF16),
            jax.ShapeDtypeStruct((2, BLOCK, width), F32),
            jax.ShapeDtypeStruct((2, ROWS, width), F32),
            jax.ShapeDtypeStruct((2, ROWS, width), F32),
            jax.ShapeDtypeStruct((2, ROWS, width), BF16),
        ],
        input_output_aliases={10: 0, 11: 1} if chain else {},
        cost_estimate=COST,
        compiler_params=pltpu.CompilerParams(vmem_limit_bytes=VMEM_LIMIT),
        name="attend",
    )(core, q, g, k, v, qg_recv, kv_recv, first, second, third, *chain, *after)


def back_second_kernel(second_ref, third_ref, *refs):
    out_ref = refs[-1]
    pairs = spreader(64, 2)
    for part in range(2):
        out_ref[part] = (second_ref[part] + dot(pairs, third_ref[part, 64:])).astype(BF16)


def back_first_kernel(first_ref, second_ref, third_ref, *refs):
    out_ref = refs[-1]
    pairs = spreader(64, 2)
    fours = spreader(32, 4)
    for part in range(2):
        out_ref[part] = (
            first_ref[part]
            + dot(pairs, second_ref[part, 64:])
            + dot(fours, third_ref[part, 32:64])
        ).astype(BF16)


def finish_kernel(start, heads, exact_ref, first_ref, second_ref, third_ref, *refs):
    own_out, peer_out, token, total_ref, sems = refs[-5:]
    token[...] = jnp.zeros_like(token)
    weights = jnp.concatenate(
        [spreader(128, 2), spreader(64, 4), spreader(32, 8)], axis=1
    )
    for part in range(2):
        rows = jnp.concatenate(
            [first_ref[part], second_ref[part, :64], third_ref[part, :32]], axis=0
        )
        total_ref[part] = (exact_ref[part] + dot(weights, rows)).astype(BF16)
    lanes = pl.ds(start * HEAD_DIM, heads * HEAD_DIM)
    copies = [
        pltpu.make_async_copy(
            total_ref.at[:, pl.ds(part * ROWS, ROWS)], out.at[:, :, lanes], sems.at[part]
        )
        for part, out in enumerate((own_out, peer_out))
    ]
    for copy in copies:
        copy.start()
    for copy in copies:
        copy.wait()


def finish(start, heads, exact, first, second, third, chain, after):
    in_vmem = pl.BlockSpec(memory_space=pltpu.VMEM)
    chain = list(chain) if chain is not None else []
    return pl.pallas_call(
        functools.partial(finish_kernel, start, heads),
        in_specs=[in_vmem] * 4 + [ANYWHERE] * (len(chain) + len(after)),
        out_specs=[ANYWHERE, ANYWHERE, in_vmem],
        out_shape=[jax.ShapeDtypeStruct((2, ROWS, HALF), BF16)] * 2
        + [jax.ShapeDtypeStruct((8, 128), F32)],
        scratch_shapes=[
            pltpu.VMEM((2, BLOCK, heads * HEAD_DIM), BF16),
            pltpu.SemaphoreType.DMA((2,)),
        ],
        input_output_aliases={4: 0, 5: 1} if chain else {},
        cost_estimate=COST,
        compiler_params=pltpu.CompilerParams(vmem_limit_bytes=VMEM_LIMIT),
        name="finish",
    )(exact, first, second, third, *chain, *after)


def assemble_kernel(core, own_ref, recv_ref, *refs):
    a_ref, b_ref, token = refs[-3:]
    token[...] = jnp.zeros_like(token)
    mine = pl.program_id(0) == core[0]

    @pl.when(mine)
    def _():
        a_ref[...] = own_ref[0]
        b_ref[...] = own_ref[1]

    @pl.when(jnp.logical_not(mine))
    def _():
        a_ref[...] = recv_ref[0]
        b_ref[...] = recv_ref[1]


def assemble(core, own, recv, after):
    whole = pl.BlockSpec((2, ROWS, HALF), lambda j, c: (0, 0, 0))
    half = pl.BlockSpec((ROWS, HALF), lambda j, c: (0, j))
    return pl.pallas_call(
        assemble_kernel,
        grid_spec=pltpu.PrefetchScalarGridSpec(
            num_scalar_prefetch=1, grid=(2,), in_specs=[whole, whole] + [ANYWHERE] * len(after),
            out_specs=[half, half, pl.BlockSpec((8, 128), lambda j, c: (0, 0))],
        ),
        out_shape=[jax.ShapeDtypeStruct((ROWS, 2 * HALF), BF16)] * 2
        + [jax.ShapeDtypeStruct((8, 128), F32)],
        cost_estimate=COST,
        compiler_params=params(),
        name="assemble",
    )(core, own, recv, *after)


def swap_core(block):
    return lax.ppermute(block, "fine", [(i, i ^ 1) for i in range(lax.axis_size("fine"))])


def swap_fine(block, mask):
    return lax.ppermute(block, "fine", [(i, i ^ mask) for i in range(lax.axis_size("fine"))])


def swap_next(block, odd):
    fine, coarse = lax.axis_size("fine"), lax.axis_size("coarse")
    route = []
    for f in range(fine):
        for c in range(coarse):
            z = (f // 2) * 2 + c % 2
            if odd:
                there = (z + 1 if z % 2 else z - 1) % fine
            else:
                there = z ^ 1
            route.append((f * coarse + c, (there // 2 * 2 + f % 2) * coarse + c - c % 2 + there % 2))
    return lax.ppermute(block, ("fine", "coarse"), route)


def body(query_rows, key_rows, value_rows, out_grad):
    full_shape = query_rows.shape
    queries, keys, values, grads = (
        block.reshape(ROWS, 2 * HALF) for block in (query_rows, key_rows, value_rows, out_grad)
    )
    core = (lax.axis_index("fine") % 2).astype(jnp.int32).reshape(1)
    count = len(CHUNKS)
    starts = [sum(CHUNKS[:n]) for n in range(count)]
    own_packed, first, second, third = ([None] * count for _ in range(4))
    results, third_back, second_back, first_back = ([None] * count for _ in range(4))
    a_chain, b_chain, a_recv, after = None, None, None, []

    def shape_of(n):
        return jax.ShapeDtypeStruct((2, ROWS, CHUNKS[n] * HEAD_DIM), BF16)

    for step in ORDER:
        kind, n = step[0], int(step[1:])
        if kind == "K":
            send = extract_other(core, keys, values, after, VMEM_LIMIT)
            kv_recv = swap_core(send)
        elif kind == "Q":
            send = extract_other(core, queries, grads, after, VMEM_LIMIT)
            qg_recv = swap_core(send)
        elif kind == "A":
            packed = pack_first(core, keys, values, kv_recv, after)
            own_packed = packed[1::2]
            first = [swap_fine(rows, 2) for rows in packed[::2]]
            send = packed[0]
        elif kind == "B":
            send = whole_call(
                pack_second_kernel, "pack_second", shape_of(n), after, own_packed[n], first[n]
            )
            second[n] = swap_fine(send, 6)
        elif kind == "D":
            send = whole_call(
                pack_third_kernel, "pack_third", shape_of(n), after, own_packed[n], first[n], second[n]
            )
            third[n] = swap_next(send, PARITY[n])
        elif kind == "E":
            results[n] = attend(
                core, starts[n], CHUNKS[n], queries, grads, keys, values, qg_recv, kv_recv,
                first[n], second[n], third[n], a_chain, after,
            )
            a_chain = results[n][:2]
            send = results[n][5]
            third_back[n] = swap_next(send, PARITY[n])
        elif kind == "F":
            send = whole_call(
                back_second_kernel, "back_second", shape_of(n), after, results[n][4], third_back[n]
            )
            second_back[n] = swap_fine(send, 6)
        elif kind == "G":
            send = whole_call(
                back_first_kernel, "back_first", shape_of(n), after,
                results[n][3], second_back[n], third_back[n],
            )
            first_back[n] = swap_fine(send, 2)
        elif kind == "H":
            *b_chain, send = finish(
                starts[n], CHUNKS[n], results[n][2], first_back[n], second_back[n], third_back[n],
                b_chain, after,
            )
        elif kind == "S":
            a_recv = swap_core(a_chain[1])
            continue
        elif kind == "R":
            after = after + [qg_recv]
            continue
        elif kind == "T":
            attended, query_grad, send = assemble(core, a_chain[0], a_recv, after)
        after = [send]
    b_recv = swap_core(b_chain[1])
    key_grad, value_grad, _ = assemble(core, b_chain[0], b_recv, after)
    return tuple(
        block.reshape(full_shape) for block in (attended, query_grad, key_grad, value_grad)
    )


def solution(mesh):
    placed = P("coarse", "fine", None, None)
    return jax.shard_map(
        body, mesh=mesh, in_specs=(placed,) * 4, out_specs=(placed,) * 4, check_vma=False
    )
```

```python
import functools
import math

import jax
import jax.numpy as jnp
from jax import lax
from jax.experimental import pallas as pl
from jax.experimental.pallas import tpu as pltpu
from jax.sharding import PartitionSpec as P

HEADS = 24
HEAD_DIM = 128
ROWS = 128
BLOCK = 256
CORE_HEADS = HEADS // 2
HALF = CORE_HEADS * HEAD_DIM
SCALE = HEAD_DIM**-0.5
EXP2_SCALE = SCALE * math.log2(math.e)
COST = pl.CostEstimate(flops=1, bytes_accessed=1, transcendentals=0)
CHUNKS = (3, 3, 3, 3)
PARITY = (0, 0, 0, 1)
ORDER = (
    "K0", "Q0", "A0", "B1", "B2", "D1", "B3", "D2", "B0", "E1",
    "D3", "D0", "E2", "F1", "E3", "E0", "G1", "F2", "F3", "F0",
    "S0", "R0", "G2", "H1", "G0", "H2", "G3", "H0", "T0", "H3",
)
VMEM_LIMIT = 40 * 2**20
BF16 = jnp.bfloat16
F32 = jnp.float32
ANYWHERE = pl.BlockSpec(memory_space=pl.ANY)


def params(steps=1):
    return pltpu.CompilerParams(
        dimension_semantics=("arbitrary",) * steps, vmem_limit_bytes=VMEM_LIMIT
    )


def averager(rows, group):
    row = lax.broadcasted_iota(jnp.int32, (rows, rows * group), 0)
    col = lax.broadcasted_iota(jnp.int32, (rows, rows * group), 1)
    return jnp.where(col // group == row, 1.0 / group, 0.0).astype(BF16)


def spreader(rows, group):
    row = lax.broadcasted_iota(jnp.int32, (rows * group, rows), 0)
    col = lax.broadcasted_iota(jnp.int32, (rows * group, rows), 1)
    return jnp.where(row // group == col, 1.0 / group, 0.0).astype(BF16)


def dot(a, b, dims=((1,), (0,))):
    return lax.dot_general(a, b, (dims, ((), ())), preferred_element_type=F32)


def extract_kernel(core, a_ref, b_ref, *refs):
    out_ref = refs[-1]
    out_ref[0] = a_ref[...]
    out_ref[1] = b_ref[...]


def extract_other(core, a, b, after, limit):
    half = pl.BlockSpec((ROWS, HALF), lambda i, c: (0, 1 - c[0]))
    return pl.pallas_call(
        extract_kernel,
        grid_spec=pltpu.PrefetchScalarGridSpec(
            num_scalar_prefetch=1,
            grid=(1,),
            in_specs=[half, half] + [ANYWHERE] * len(after),
            out_specs=pl.BlockSpec((2, ROWS, HALF), lambda i, c: (0, 0, 0)),
        ),
        out_shape=jax.ShapeDtypeStruct((2, ROWS, HALF), BF16),
        cost_estimate=COST,
        compiler_params=pltpu.CompilerParams(vmem_limit_bytes=limit),
        name="extract_other",
    )(core, a, b, *after)


def pack_first_kernel(core, k_ref, v_ref, kv_ref, *refs):
    outs = refs[-2 * len(CHUNKS) :]
    weights = jnp.concatenate(
        [averager(BLOCK >> level, 1 << level) for level in (1, 2, 3)], axis=0
    )
    for part, own in enumerate((k_ref, v_ref)):
        rows = jnp.concatenate([own[...], kv_ref[part]], axis=0)
        lane = 0
        for number, heads in enumerate(CHUNKS):
            width = heads * HEAD_DIM
            coarse = dot(weights, rows[:, lane : lane + width]).astype(BF16)
            outs[2 * number][part] = coarse[:128]
            outs[2 * number + 1][part] = coarse[128:]
            lane += width


def pack_first(core, keys, values, kv_recv, after):
    half = pl.BlockSpec((ROWS, HALF), lambda i, c: (0, c[0]))
    whole = pl.BlockSpec((2, ROWS, HALF), lambda i, c: (0, 0, 0))
    shapes = [(2, count, heads * HEAD_DIM) for heads in CHUNKS for count in (128, 96)]
    return pl.pallas_call(
        pack_first_kernel,
        grid_spec=pltpu.PrefetchScalarGridSpec(
            num_scalar_prefetch=1,
            grid=(1,),
            in_specs=[half, half, whole] + [ANYWHERE] * len(after),
            out_specs=[pl.BlockSpec(shape, lambda i, c: (0, 0, 0)) for shape in shapes],
        ),
        out_shape=[jax.ShapeDtypeStruct(shape, BF16) for shape in shapes],
        cost_estimate=COST,
        compiler_params=params(),
        name="pack_first",
    )(core, keys, values, kv_recv, *after)


def whole_call(kernel, name, out_shape, after, *args):
    return pl.pallas_call(
        kernel,
        in_specs=[pl.BlockSpec(memory_space=pltpu.VMEM)] * len(args) + [ANYWHERE] * len(after),
        out_specs=pl.BlockSpec(memory_space=pltpu.VMEM),
        out_shape=out_shape,
        cost_estimate=COST,
        compiler_params=pltpu.CompilerParams(vmem_limit_bytes=VMEM_LIMIT),
        name=name,
    )(*args, *after)


def pack_second_kernel(own_ref, first_ref, *refs):
    out_ref = refs[-1]
    pairs = averager(64, 2)
    for part in range(2):
        out_ref[part, :64] = own_ref[part, :64]
        out_ref[part, 64:] = dot(pairs, first_ref[part]).astype(BF16)


def pack_third_kernel(own_ref, first_ref, second_ref, *refs):
    out_ref = refs[-1]
    fours = averager(32, 4)
    pairs = averager(64, 2)
    for part in range(2):
        out_ref[part, :32] = own_ref[part, 64:]
        out_ref[part, 32:64] = dot(fours, first_ref[part]).astype(BF16)
        out_ref[part, 64:] = dot(pairs, second_ref[part]).astype(BF16)


def attend_kernel(start, heads, core, q_own, g_own, k_own, v_own, *refs):
    for head in range(heads):
        attend_head(start, head, core, q_own, g_own, k_own, v_own, *refs)


def attend_head(
    start, head, core, q_own, g_own, k_own, v_own, qg_recv, kv_recv, first, second, third, *refs
):
    own_out, peer_out, exact_out, first_out, second_out, third_out = refs[-6:]
    own = pl.ds(pl.multiple_of(core[0] * HALF + (start + head) * HEAD_DIM, HEAD_DIM), HEAD_DIM)
    recv = pl.ds((start + head) * HEAD_DIM, HEAD_DIM)
    local = pl.ds(head * HEAD_DIM, HEAD_DIM)
    queries = jnp.concatenate([q_own[:, own], qg_recv[0, :, recv]], axis=0)
    grads = jnp.concatenate([g_own[:, own], qg_recv[1, :, recv]], axis=0)
    keys, values = (
        jnp.concatenate(
            [mine[:, own], kv_recv[part, :, recv]]
            + [rows[part, :, local] for rows in (first, second, third)],
            axis=0,
        )
        for part, mine in enumerate((k_own, v_own))
    )
    scores = dot(keys, queries, ((1,), (1,)))
    prob_grad = dot(values, grads, ((1,), (1,)))
    pieces = [slice(low, low + ROWS) for low in range(0, 5 * ROWS, ROWS)]

    def fold(block):
        return block.reshape(ROWS // 8, 8, BLOCK)

    tops = [jnp.max(fold(scores[piece]), axis=0) for piece in pieces]
    row_max = jnp.max(functools.reduce(jnp.maximum, tops), axis=0, keepdims=True)
    exp_scores, exp_sum, exp_grad = [], 0.0, 0.0
    for piece in pieces:
        block = jnp.exp2((scores[piece] - row_max) * EXP2_SCALE)
        exp_scores.append(block)
        exp_sum += jnp.sum(fold(block), axis=0)
        exp_grad += jnp.sum(fold(block * prob_grad[piece]), axis=0)
    inverse = 1.0 / jnp.sum(exp_sum, axis=0, keepdims=True)
    row_inner = jnp.sum(exp_grad, axis=0, keepdims=True) * inverse
    weights_low, score_grad = [], []
    for piece, block in zip(pieces, exp_scores):
        weights = block * inverse
        weights_low.append(weights.astype(BF16))
        score_grad.append((weights * (prob_grad[piece] - row_inner)).astype(BF16))
    weights_low = jnp.concatenate(weights_low, axis=0)
    score_grad = jnp.concatenate(score_grad, axis=0)
    attended = dot(values.T, weights_low).T
    query_grad = dot(keys.T, score_grad).T * SCALE
    for part, result in enumerate((attended, query_grad)):
        result = result.astype(BF16)
        own_out[part, :, recv] = result[:ROWS]
        peer_out[part, :, recv] = result[ROWS:]
    key_terms = dot(score_grad, queries) * SCALE
    value_terms = dot(weights_low, grads)
    for part, terms in enumerate((key_terms, value_terms)):
        exact_out[part, :, local] = terms[:256]
        first_out[part, :, local] = terms[256:384]
        second_out[part, :, local] = terms[384:512]
        third_out[part, :, local] = terms[512:].astype(BF16)


def attend(core, start, heads, q, g, k, v, qg_recv, kv_recv, first, second, third, chain, after):
    in_vmem = pl.BlockSpec(memory_space=pltpu.VMEM)
    width = heads * HEAD_DIM
    chain = list(chain) if chain is not None else []
    return pl.pallas_call(
        functools.partial(attend_kernel, start, heads),
        in_specs=[pl.BlockSpec(memory_space=pltpu.SMEM)]
        + [in_vmem] * (9 + len(chain))
        + [ANYWHERE] * len(after),
        out_specs=[in_vmem] * 6,
        out_shape=[
            jax.ShapeDtypeStruct((2, ROWS, HALF), BF16),
            jax.ShapeDtypeStruct((2, ROWS, HALF), BF16),
            jax.ShapeDtypeStruct((2, BLOCK, width), F32),
            jax.ShapeDtypeStruct((2, ROWS, width), F32),
            jax.ShapeDtypeStruct((2, ROWS, width), F32),
            jax.ShapeDtypeStruct((2, ROWS, width), BF16),
        ],
        input_output_aliases={10: 0, 11: 1} if chain else {},
        cost_estimate=COST,
        compiler_params=pltpu.CompilerParams(vmem_limit_bytes=VMEM_LIMIT),
        name="attend",
    )(core, q, g, k, v, qg_recv, kv_recv, first, second, third, *chain, *after)


def back_second_kernel(second_ref, third_ref, *refs):
    out_ref = refs[-1]
    pairs = spreader(64, 2)
    for part in range(2):
        out_ref[part] = (second_ref[part] + dot(pairs, third_ref[part, 64:])).astype(BF16)


def back_first_kernel(first_ref, second_ref, third_ref, *refs):
    out_ref = refs[-1]
    pairs = spreader(64, 2)
    fours = spreader(32, 4)
    for part in range(2):
        out_ref[part] = (
            first_ref[part]
            + dot(pairs, second_ref[part, 64:])
            + dot(fours, third_ref[part, 32:64])
        ).astype(BF16)


def finish_kernel(start, heads, exact_ref, first_ref, second_ref, third_ref, *refs):
    own_out, peer_out, token, total_ref, sems = refs[-5:]
    token[...] = jnp.zeros_like(token)
    weights = jnp.concatenate(
        [spreader(128, 2), spreader(64, 4), spreader(32, 8)], axis=1
    )
    for part in range(2):
        rows = jnp.concatenate(
            [first_ref[part], second_ref[part, :64], third_ref[part, :32]], axis=0
        )
        total_ref[part] = (exact_ref[part] + dot(weights, rows)).astype(BF16)
    lanes = pl.ds(start * HEAD_DIM, heads * HEAD_DIM)
    copies = [
        pltpu.make_async_copy(
            total_ref.at[:, pl.ds(part * ROWS, ROWS)], out.at[:, :, lanes], sems.at[part]
        )
        for part, out in enumerate((own_out, peer_out))
    ]
    for copy in copies:
        copy.start()
    for copy in copies:
        copy.wait()


def finish(start, heads, exact, first, second, third, chain, after):
    in_vmem = pl.BlockSpec(memory_space=pltpu.VMEM)
    chain = list(chain) if chain is not None else []
    return pl.pallas_call(
        functools.partial(finish_kernel, start, heads),
        in_specs=[in_vmem] * 4 + [ANYWHERE] * (len(chain) + len(after)),
        out_specs=[ANYWHERE, ANYWHERE, in_vmem],
        out_shape=[jax.ShapeDtypeStruct((2, ROWS, HALF), BF16)] * 2
        + [jax.ShapeDtypeStruct((8, 128), F32)],
        scratch_shapes=[
            pltpu.VMEM((2, BLOCK, heads * HEAD_DIM), BF16),
            pltpu.SemaphoreType.DMA((2,)),
        ],
        input_output_aliases={4: 0, 5: 1} if chain else {},
        cost_estimate=COST,
        compiler_params=pltpu.CompilerParams(vmem_limit_bytes=VMEM_LIMIT),
        name="finish",
    )(exact, first, second, third, *chain, *after)


def assemble_kernel(core, own_ref, recv_ref, *refs):
    a_ref, b_ref, token = refs[-3:]
    token[...] = jnp.zeros_like(token)
    mine = pl.program_id(0) == core[0]

    @pl.when(mine)
    def _():
        a_ref[...] = own_ref[0]
        b_ref[...] = own_ref[1]

    @pl.when(jnp.logical_not(mine))
    def _():
        a_ref[...] = recv_ref[0]
        b_ref[...] = recv_ref[1]


def assemble(core, own, recv, after):
    whole = pl.BlockSpec((2, ROWS, HALF), lambda j, c: (0, 0, 0))
    half = pl.BlockSpec((ROWS, HALF), lambda j, c: (0, j))
    return pl.pallas_call(
        assemble_kernel,
        grid_spec=pltpu.PrefetchScalarGridSpec(
            num_scalar_prefetch=1, grid=(2,), in_specs=[whole, whole] + [ANYWHERE] * len(after),
            out_specs=[half, half, pl.BlockSpec((8, 128), lambda j, c: (0, 0))],
        ),
        out_shape=[jax.ShapeDtypeStruct((ROWS, 2 * HALF), BF16)] * 2
        + [jax.ShapeDtypeStruct((8, 128), F32)],
        cost_estimate=COST,
        compiler_params=params(),
        name="assemble",
    )(core, own, recv, *after)


def swap_core(block):
    return lax.ppermute(block, "fine", [(i, i ^ 1) for i in range(lax.axis_size("fine"))])


def swap_fine(block, mask):
    return lax.ppermute(block, "fine", [(i, i ^ mask) for i in range(lax.axis_size("fine"))])


def swap_next(block, odd):
    fine, coarse = lax.axis_size("fine"), lax.axis_size("coarse")
    route = []
    for f in range(fine):
        for c in range(coarse):
            z = (f // 2) * 2 + c % 2
            if odd:
                there = (z + 1 if z % 2 else z - 1) % fine
            else:
                there = z ^ 1
            route.append((f * coarse + c, (there // 2 * 2 + f % 2) * coarse + c - c % 2 + there % 2))
    return lax.ppermute(block, ("fine", "coarse"), route)


def body(query_rows, key_rows, value_rows, out_grad):
    full_shape = query_rows.shape
    queries, keys, values, grads = (
        block.reshape(ROWS, 2 * HALF) for block in (query_rows, key_rows, value_rows, out_grad)
    )
    core = (lax.axis_index("fine") % 2).astype(jnp.int32).reshape(1)
    count = len(CHUNKS)
    starts = [sum(CHUNKS[:n]) for n in range(count)]
    own_packed, first, second, third = ([None] * count for _ in range(4))
    results, third_back, second_back, first_back = ([None] * count for _ in range(4))
    a_chain, b_chain, a_recv, after = None, None, None, []

    def shape_of(n):
        return jax.ShapeDtypeStruct((2, ROWS, CHUNKS[n] * HEAD_DIM), BF16)

    for step in ORDER:
        kind, n = step[0], int(step[1:])
        if kind == "K":
            send = extract_other(core, keys, values, after, VMEM_LIMIT)
            kv_recv = swap_core(send)
        elif kind == "Q":
            send = extract_other(core, queries, grads, after, VMEM_LIMIT)
            qg_recv = swap_core(send)
        elif kind == "A":
            packed = pack_first(core, keys, values, kv_recv, after)
            own_packed = packed[1::2]
            first = [swap_fine(rows, 2) for rows in packed[::2]]
            send = packed[0]
        elif kind == "B":
            send = whole_call(
                pack_second_kernel, "pack_second", shape_of(n), after, own_packed[n], first[n]
            )
            second[n] = swap_fine(send, 6)
        elif kind == "D":
            send = whole_call(
                pack_third_kernel, "pack_third", shape_of(n), after, own_packed[n], first[n], second[n]
            )
            third[n] = swap_next(send, PARITY[n])
        elif kind == "E":
            results[n] = attend(
                core, starts[n], CHUNKS[n], queries, grads, keys, values, qg_recv, kv_recv,
                first[n], second[n], third[n], a_chain, after,
            )
            a_chain = results[n][:2]
            send = results[n][5]
            third_back[n] = swap_next(send, PARITY[n])
        elif kind == "F":
            send = whole_call(
                back_second_kernel, "back_second", shape_of(n), after, results[n][4], third_back[n]
            )
            second_back[n] = swap_fine(send, 6)
        elif kind == "G":
            send = whole_call(
                back_first_kernel, "back_first", shape_of(n), after,
                results[n][3], second_back[n], third_back[n],
            )
            first_back[n] = swap_fine(send, 2)
        elif kind == "H":
            *b_chain, send = finish(
                starts[n], CHUNKS[n], results[n][2], first_back[n], second_back[n], third_back[n],
                b_chain, after,
            )
        elif kind == "S":
            a_recv = swap_core(a_chain[1])
            continue
        elif kind == "R":
            after = after + [qg_recv]
            continue
        elif kind == "T":
            attended, query_grad, send = assemble(core, a_chain[0], a_recv, after)
        after = [send]
    b_recv = swap_core(b_chain[1])
    key_grad, value_grad, _ = assemble(core, b_chain[0], b_recv, after)
    return tuple(
        block.reshape(full_shape) for block in (attended, query_grad, key_grad, value_grad)
    )


def solution(mesh):
    placed = P("coarse", "fine", None, None)
    return jax.shard_map(
        body, mesh=mesh, in_specs=(placed,) * 4, out_specs=(placed,) * 4, check_vma=False
    )
```
